512 devices in a mesh: depth: 4 (over y_lo, core), row: 16 (over x, y_hi), col: 8 (over z).
Axes of the slice: x: 4, y: 8 (y_hi: 4, y_lo: 2; y = y_hi * 2 + y_lo), z: 8, core: 2. Of those that a mesh axis runs over, the one named last changes fastest.
Arguments:
- activations: bfloat16 [512, 12288], P(('depth', 'col'), 'row'), may hold values from -6 to 6
- weight_up: bfloat16 [12288, 24576], P('row', ('depth', 'col')), may hold values from -0.0546875 to 0.0546875
- weight_down: bfloat16 [24576, 12288], P(('depth', 'col'), 'row'), may hold values from -0.0390625 to 0.0390625
- out_grad: bfloat16 [512, 12288], P(('depth', 'col'), 'row'), may hold values from -6 to 6
Outputs:
- layer_out: bfloat16 [512, 12288], P(('depth', 'col'), 'row')
- input_grad: bfloat16 [512, 12288], P(('depth', 'col'), 'row')
- up_grad: bfloat16 [12288, 24576], P('row', ('depth', 'col'))
- down_grad: bfloat16 [24576, 12288], P(('depth', 'col'), 'row')
The draws below stay inside these ranges and needn't reach their ends.
All inputs are finite; a program needn't handle non-finite values.
Results may differ from the reference program's by a relative error of at most 0.0049.
Values may be sent and summed in bfloat16 or wider, within the bound.
A program may use at most 64 MiB of HBM per device.

```python
import jax
import jax.numpy as jnp
from jax import lax

D = 12288
FF = 24576
TOKENS = 512


def block_scale(key, shape, pieces, low, top_value):
    factor_of = 1.0
    for dim, shards_of in pieces:
        steps = jax.random.uniform(jax.random.fold_in(jax.random.fold_in(key, 6), dim), (shards_of,), jnp.float32, low / len(pieces), top_value / len(pieces))
        factor_of = factor_of * jnp.repeat(jnp.exp(steps), shape[dim] // shards_of).reshape((-1,) + (1,) * (len(shape) - 1 - dim))
    return factor_of


def gaussian(own_key, dims, spread, bound, shards=(), kind=jnp.bfloat16):
    array = spread * jax.random.normal(own_key, dims, jnp.float32)
    if shards:
        array = array * block_scale(own_key, dims, shards, -0.22, 0.18)
    return jnp.clip(array, -bound, bound).astype(kind)


def setup_inputs(seed: int = 0) -> dict:
    key_list = jax.random.split(jax.random.key(seed), 5)
    activations = gaussian(key_list[0], (TOKENS, D), 1.0, 6.0, ((0, 32), (1, 16)))
    weight_up = gaussian(key_list[1], (D, FF), D ** -0.5, 0.0546875, ((0, 16), (1, 32)))
    weight_down = gaussian(key_list[2], (FF, D), FF ** -0.5, 0.0390625, ((0, 32), (1, 16)))
    out_grad = gaussian(key_list[3], (TOKENS, D), 1.0, 6.0, ((0, 32), (1, 16)))
    return dict(activations=activations, weight_up=weight_up, weight_down=weight_down, out_grad=out_grad)


tanh_scale = 0.7978845608028654
cubic_coeff = 0.044715


def gelu_parts(preact):
    inner = tanh_scale * (preact + cubic_coeff * preact * preact * preact)
    hyper = jnp.tanh(inner)
    activated = 0.5 * preact * (1.0 + hyper)
    derivative = 0.5 * (1.0 + hyper) + 0.5 * preact * (1.0 - hyper * hyper) * tanh_scale * (1.0 + 3.0 * cubic_coeff * preact * preact)
    return activated, derivative


def contract(left, right, left_dim, right_dim):
    return lax.dot_general(left, right, (((left_dim,), (right_dim,)), ((), ())), preferred_element_type=jnp.float32)


def reference(activations, weight_up, weight_down, out_grad):
    preact = jnp.dot(activations, weight_up, preferred_element_type=jnp.float32)
    activated, derivative = gelu_parts(preact)
    hidden = activated.astype(jnp.bfloat16)
    layer_out = jnp.dot(hidden, weight_down, preferred_element_type=jnp.float32).astype(jnp.bfloat16)
    backed = contract(out_grad, weight_down, 1, 1)
    pre_grad = (backed * derivative).astype(jnp.bfloat16)
    input_grad = contract(pre_grad, weight_up, 1, 1).astype(jnp.bfloat16)
    up_grad = contract(activations, pre_grad, 0, 0).astype(jnp.bfloat16)
    down_grad = contract(hidden, out_grad, 0, 0).astype(jnp.bfloat16)
    return (layer_out, input_grad, up_grad, down_grad)
```

```python
import jax
import jax.numpy as jnp
from jax import lax
from jax.experimental import pallas as pl
from jax.experimental.pallas import tpu as pltpu
from jax.sharding import PartitionSpec as P

tanh_scale = 0.7978845608028654
cubic_coeff = 0.044715

OFFSETS = (0, 1, -1, 2, -2, 3, -3, 4)
CHUNKS = 4
BLK = 16


def slot_of(offset):
    return OFFSETS.index(4 if offset == -4 else offset)


def gelu_parts(preact):
    inner = tanh_scale * (preact + cubic_coeff * preact * preact * preact)
    hyper = jnp.tanh(inner)
    activated = 0.5 * preact * (1.0 + hyper)
    derivative = 0.5 * (1.0 + hyper) + 0.5 * preact * (1.0 - hyper * hyper) * tanh_scale * (
        1.0 + 3.0 * cubic_coeff * preact * preact
    )
    return (activated, derivative)


def contract(left, right, left_dim, right_dim):
    return lax.dot_general(
        left, right, (((left_dim,), (right_dim,)), ((), ())), preferred_element_type=jnp.float32
    )


def rows_of(value):
    return value.reshape((-1, value.shape[-1]))


def kernel(
    act_hbm, up_hbm, down_hbm, cot_hbm,
    out_hbm, in_grad_hbm, up_grad_hbm, down_grad_hbm,
    tok, w_up, w_down, acc0, s1, r1, acc2, s2, r2, acc3, s3, r3, acc4, s4, r4,
    hp, part, q0, ky, sy, ry, own, ds, rd, up_out, down_out, small_out,
    load_sem, store_sem, send_sem, recv_sem,
):
    bf16, f32 = jnp.bfloat16, jnp.float32
    width = tok.shape[-1]
    half = width // 2
    depth, row, z = lax.axis_index("depth"), lax.axis_index("row"), lax.axis_index("col")
    yl, k = depth // 2, depth % 2
    x, yh = row // 4, row % 4
    f1x, f2x = (x + x // 2) % 2, x // 2
    f1y, f2y = (yh + yh // 2) % 2, yh // 2
    p1x, p2x = {"row": (x + 1 - 2 * (x % 2)) * 4 + yh}, {"row": (3 - x) * 4 + yh}
    p1y, p2y = {"row": x * 4 + yh + 1 - 2 * (yh % 2)}, {"row": x * 4 + 3 - yh}
    sibling, ypartner = {"depth": yl * 2 + 1 - k}, {"depth": (1 - yl) * 2 + k}

    def along(offset):
        return {"col": (z + offset + 8) % 8}

    partners = [sibling, ypartner, p1x, p2x, p1y, p2y] + [along(o) for o in OFFSETS[1:]]

    started = []

    def send(src, dst, device):
        n = len(started)
        copy = pltpu.make_async_remote_copy(
            src_ref=src, dst_ref=dst, send_sem=send_sem.at[n], recv_sem=recv_sem.at[n],
            device_id=device, device_id_type=pl.DeviceIdType.MESH,
        )
        copy.start()
        started.append(copy)
        return copy

    loads = [
        pltpu.make_async_copy(act_hbm, tok.at[0, 0, k, yl], load_sem.at[0]),
        pltpu.make_async_copy(cot_hbm, tok.at[1, 0, k, yl], load_sem.at[1]),
        pltpu.make_async_copy(up_hbm, w_up, load_sem.at[2]),
        pltpu.make_async_copy(down_hbm, w_down, load_sem.at[3]),
    ]
    for load in loads:
        load.start()
    barrier = pltpu.get_barrier_semaphore()
    for device in partners:
        pl.semaphore_signal(barrier, inc=1, device_id=device, device_id_type=pl.DeviceIdType.MESH)
    pl.semaphore_wait(barrier, len(partners))

    flow, across, shared = {}, {}, {}

    def block(slot, a=slice(None)):
        return tok.at[a, slot, k, yl]

    def hop(offset, way, a=slice(None)):
        target = offset - way
        flow[target] = flow.get(target, []) + [
            send(block(slot_of(offset), a), block(slot_of(target), a), along(way))
        ]

    def cross(slot):
        across[slot] = send(block(slot), block(slot), ypartner)

    def arrive(offset):
        for copy in flow[offset]:
            copy.wait_recv()

    def share(slot):
        across[slot].wait_recv()
        mine = tok.at[:, slot, k]
        shared[slot] = send(mine, mine, sibling)

    wave = {}

    def reduce1(c):
        for slot in (2 * c, 2 * c + 1):
            shared[slot].wait_recv()
        for a in range(2):
            i, f = 2 * c + a, (f1x, f2x)[a]
            rows = rows_of(tok[a, 2 * c : 2 * c + 2])
            value = contract(rows, w_up[...], 1, 0) if a == 0 else contract(rows, w_down[...], 1, 1)
            acc0[i] = value.reshape(acc0.shape[1:])
            s1[i] = (acc0[i, 1 - f] if a == 0 else acc0[i, :, 1 - f]).astype(bf16)
            wave[c, a] = send(s1.at[i], r1.at[i], (p1x, p2x)[a])

    def reduce2(c):
        for a in range(2):
            i, f, g = 2 * c + a, (f1x, f2x)[a], (f2x, f1x)[a]
            wave[c, a].wait_recv()

            def total(n):
                kept = acc0[i, f, n] if a == 0 else acc0[i, n, f]
                return kept + r1[i, n].astype(f32)

            value = total(1 - g).astype(bf16)
            s2[i, :, 0] = value[..., :half]
            s2[i, :, 1] = value[..., half:]
            wave[c, a] = send(s2.at[i], r2.at[i], (p2x, p1x)[a])
            value = total(g)
            acc2[i, :, 0] = value[..., :half]
            acc2[i, :, 1] = value[..., half:]

    def reduce3(c):
        for a in range(2):
            i, f = 2 * c + a, (f1y, f2y)[a]
            wave[c, a].wait_recv()

            def total(n):
                if a == 0:
                    return acc2[i, n] + r2[i, n].astype(f32)
                return acc2[i, :, n] + r2[i, :, n].astype(f32)

            s3[i] = total(1 - f).astype(bf16)
            wave[c, a] = send(s3.at[i], r3.at[i], (p1y, p2y)[a])
            acc3[i] = total(f)

    def reduce4(c):
        for a in range(2):
            i, f = 2 * c + a, (f2y, f1y)[a]
            wave[c, a].wait_recv()
            s4[i] = acc3[i, 1 - f] + r3[i, 1 - f].astype(f32)
            wave[c, a] = send(s4.at[i], r4.at[i], (p2y, p1y)[a])
            acc4[i] = acc3[i, f] + r3[i, f].astype(f32)

    def double(c, step):
        for a in range(2):
            if step > 0:
                wave[c, a].wait_recv()
            if step == 0:
                region, device = hp.at[c, a, f1x, f2x, f1y, f2y], (p2y, p1y)[a]
            elif step == 1:
                region = hp.at[c, a, f1x, f2x, f1y] if a == 0 else hp.at[c, a, f1x, f2x, :, f2y]
                device = (p1y, p2y)[a]
            elif step == 2:
                region, device = hp.at[c, a, f1x, f2x], (p2x, p1x)[a]
            else:
                region = hp.at[c, a, f1x] if a == 0 else hp.at[c, a, :, f2x]
                device = (p1x, p2x)[a]
            wave[c, a] = send(region, region, device)

    def activate(c):
        wave[c, 0].wait_recv()
        wave[c, 1].wait_recv()
        activated, derivative = gelu_parts(acc4[2 * c] + r4[2 * c])
        hp[c, 0, f1x, f2x, f1y, f2y] = activated.astype(bf16)
        backed = acc4[2 * c + 1] + r4[2 * c + 1]
        hp[c, 1, f1x, f2x, f1y, f2y] = (backed * derivative).astype(bf16)
        double(c, 0)

    pair, cut, scattered = {}, {}, []

    def project(c):
        for a in range(2):
            wave[c, a].wait_recv()
            low, high = rows_of(hp[c, a, :, :, :, 0]), rows_of(hp[c, a, :, :, :, 1])
            rows = jnp.concatenate([low, high], axis=1)
            value = contract(rows, w_down[...], 1, 0) if a == 0 else contract(rows, w_up[...], 1, 1)
            part[c, a] = value.reshape(part.shape[2:])
            pair[c, a] = send(part.at[c, a, :, 1 - k], q0.at[c, a], sibling)

    def merge(c):
        for a in range(2):
            pair[c, a].wait_recv()
            sy[c, a] = (part[c, a, :, k, 1 - yl] + q0[c, a, :, 1 - yl]).astype(bf16)
        cut[c] = send(sy.at[c], ry.at[c], ypartner)
        for a in range(2):
            ky[c, a] = part[c, a, :, k, yl] + q0[c, a, :, yl]

    def scatter(c):
        cut[c].wait_recv()
        for s in (1, 0):
            slot = 2 * c + s
            value = ky[c, :, s] + ry[c, :, s].astype(f32)
            if slot == 0:
                own[...] = value
            else:
                ds[slot] = value.astype(bf16)
                scattered.append(send(ds.at[slot], rd.at[slot], along(OFFSETS[slot])))

    stores = []

    def store(src, dst):
        stores.append(pltpu.make_async_copy(src, dst, store_sem.at[len(stores)]))
        stores[-1].start()

    def up_grad(h):
        cols = slice(h * half, (h + 1) * half)
        left, right = rows_of(tok[0]), rows_of(hp[:, 1, :, :, :, h])
        up_out[:, cols] = contract(left, right, 0, 0).astype(bf16)
        store(up_out.at[:, cols], up_grad_hbm.at[:, cols])

    def down_grad(h):
        rows = slice(h * half, (h + 1) * half)
        left, right = rows_of(hp[:, 0, :, :, :, h]), rows_of(tok[1])
        down_out[rows, :] = contract(left, right, 0, 0).astype(bf16)
        store(down_out.at[rows], down_grad_hbm.at[rows])

    loads[0].wait()
    loads[1].wait()
    hop(0, 1)
    hop(0, -1)
    cross(0)
    hop(0, 2)
    hop(0, -2)
    share(0)
    for offset in (1, -1):
        arrive(offset)
        cross(slot_of(offset))
    for offset in (-2, 2):
        way = -offset // 2
        arrive(offset)
        hop(offset, way)
        hop(offset, 2 * way, 0 if way == 1 else 1)
        cross(slot_of(offset))
    share(1)
    loads[2].wait()
    loads[3].wait()
    reduce1(0)
    share(2)
    share(3)
    for offset in (3, -3, 4):
        arrive_keys = (4, -4) if offset == 4 else (offset,)
        for key in arrive_keys:
            arrive(key)
        cross(slot_of(offset))
    stages = [
        reduce1, reduce2, reduce3, reduce4, activate,
        lambda c: double(c, 1), lambda c: double(c, 2), lambda c: double(c, 3),
        project, merge, scatter,
    ]
    last = CHUNKS - 1
    for t in range(1, len(stages) + last):
        for c in range(CHUNKS):
            n = t - c
            if n == 0 and c >= 2:
                share(2 * c)
                share(2 * c + 1)
            if 0 <= n < len(stages):
                stages[n](c)
                if c == last and stages[n] is project:
                    up_grad(0)
                if c == last and stages[n] is merge:
                    up_grad(1)
                    down_grad(0)
    down_grad(1)
    for copy in scattered:
        copy.wait_recv()
    for a, ref in ((0, out_hbm), (1, in_grad_hbm)):
        total = own[a]
        for slot in range(1, 8):
            total = total + rd[slot, a].astype(f32)
        small_out[a] = total.astype(bf16)
        store(small_out.at[a], ref)
    for copy in started:
        copy.wait_send()
    for copy in stores:
        copy.wait()


COPIES = 128


def place(*refs):
    half = (len(refs) - 1) // 2
    copies = [
        pltpu.make_async_copy(src, dst, refs[-1].at[n])
        for n, (src, dst) in enumerate(zip(refs[:half], refs[half:-1]))
    ]
    for copy in copies:
        copy.start()
    for copy in copies:
        copy.wait()


def shards(activations, weight_up, weight_down, out_grad):
    width, hidden = weight_up.shape
    bf16, f32 = jnp.bfloat16, jnp.float32
    assert activations.shape[0] == BLK and width == hidden

    def vmem(lead, kind):
        return pltpu.VMEM(lead + (BLK, width), kind)

    def halves(lead, kind):
        return pltpu.VMEM(lead + (BLK, hidden // 2), kind)

    pieces = 2 * CHUNKS
    scratch = [
        vmem((2, 8, 2, 2), bf16),
        pltpu.VMEM((width, hidden), bf16), pltpu.VMEM((width, hidden), bf16),
        vmem((pieces, 2, 2, 2), f32), vmem((pieces, 2, 2), bf16), vmem((pieces, 2, 2), bf16),
        halves((pieces, 2, 2), f32), halves((pieces, 2, 2), bf16), halves((pieces, 2, 2), bf16),
        halves((pieces, 2), f32), halves((pieces, 2), bf16), halves((pieces, 2), bf16),
        halves((pieces,), f32), halves((pieces,), f32), halves((pieces,), f32),
        halves((CHUNKS, 2, 2, 2, 2, 2), bf16),
        vmem((CHUNKS, 2, 2, 2, 2), f32), vmem((CHUNKS, 2, 2, 2), f32),
        vmem((CHUNKS, 2, 2), f32), vmem((CHUNKS, 2, 2), bf16), vmem((CHUNKS, 2, 2), bf16),
        vmem((2,), f32), vmem((8, 2), bf16), vmem((8, 2), bf16),
        pltpu.VMEM((width, hidden), bf16), pltpu.VMEM((width, hidden), bf16), vmem((2,), bf16),
        pltpu.SemaphoreType.DMA((4,)), pltpu.SemaphoreType.DMA((6,)),
        pltpu.SemaphoreType.DMA((COPIES,)),
        pltpu.SemaphoreType.DMA((COPIES,)),
    ]
    small = jax.ShapeDtypeStruct(activations.shape, bf16)
    large = jax.ShapeDtypeStruct(weight_up.shape, bf16)
    results = pl.pallas_call(
        kernel,
        out_shape=(small, small, large, large),
        in_specs=[pl.BlockSpec(memory_space=pltpu.HBM)] * 4,
        out_specs=[pl.BlockSpec(memory_space=pltpu.HBM)] * 4,
        scratch_shapes=scratch,
        compiler_params=pltpu.CompilerParams(
            collective_id=0, has_side_effects=True, vmem_limit_bytes=VMEM_MIB * 1024 * 1024
        ),
        cost_estimate=pl.CostEstimate(
            flops=12 * 512 * width * hidden, bytes_accessed=8 * width * hidden, transcendentals=0
        ),
        name="layer",
    )(activations, weight_up, weight_down, out_grad)
    return pl.pallas_call(
        place,
        out_shape=(small, small, large, large),
        in_specs=[pl.BlockSpec(memory_space=pltpu.HBM)] * 4,
        out_specs=[pl.BlockSpec(memory_space=pltpu.HBM)] * 4,
        scratch_shapes=[pltpu.SemaphoreType.DMA((4,))],
        compiler_params=pltpu.CompilerParams(vmem_limit_bytes=VMEM_MIB * 1024 * 1024),
        name="place",
    )(*results)


VMEM_MIB = 60


def solution(mesh):
    placed = (
        P(("depth", "col"), "row"),
        P("row", ("depth", "col")),
        P(("depth", "col"), "row"),
        P(("depth", "col"), "row"),
    )
    return jax.shard_map(
        shards,
        mesh=mesh,
        in_specs=placed,
        out_specs=(
            P(("depth", "col"), "row"),
            P(("depth", "col"), "row"),
            P("row", ("depth", "col")),
            P(("depth", "col"), "row"),
        ),
        check_vma=False,
    )
```

```python
import jax
import jax.numpy as jnp
from jax import lax
from jax.experimental import pallas as pl
from jax.experimental.pallas import tpu as pltpu
from jax.sharding import PartitionSpec as P

tanh_scale = 0.7978845608028654
cubic_coeff = 0.044715

OFFSETS = (0, 1, -1, 2, -2, 3, -3, 4)
CHUNKS = 4
BLK = 16


ORDER = (
    ("y", 1), ("s", 0), ("y", -1), ("s", 1), ("y", 2), ("y", -2), ("s", 2),
    ("r1", 0), ("s", 3), ("y", 3), ("r1", 1), ("y", 4), ("y", -3), ("s", 4),
    ("s", 5), ("r2", 0), ("r1", 2), ("s", 6), ("s", 7), ("r2", 1), ("r3", 0),
    ("r1", 3), ("r2", 2), ("r3", 1), ("r4", 0), ("r2", 3), ("r3", 2), ("r4", 1),
    ("r3", 3), ("r4", 2), ("act", 1), ("r4", 3), ("act", 2), ("c1", 1), ("act", 0),
    ("c1", 2), ("c2", 1), ("act", 3), ("c2", 2), ("c3", 1), ("c1", 3), ("c3", 2),
    ("c1", 0), ("c2", 3), ("p", 1), ("c2", 0), ("p", 2), ("c3", 3), ("m", 1),
    ("c3", 0), ("m", 2), ("p", 3), ("z", 1), ("p", 0), ("z", 2), ("m", 3),
    ("g", 3), ("g", 1), ("m", 0), ("z", 3), ("g", 0), ("g", 2), ("z", 0),
)


def slot_of(offset):
    return OFFSETS.index(4 if offset == -4 else offset)


def gelu_parts(preact):
    inner = tanh_scale * (preact + cubic_coeff * preact * preact * preact)
    hyper = jnp.tanh(inner)
    activated = 0.5 * preact * (1.0 + hyper)
    derivative = 0.5 * (1.0 + hyper) + 0.5 * preact * (1.0 - hyper * hyper) * tanh_scale * (
        1.0 + 3.0 * cubic_coeff * preact * preact
    )
    return (activated, derivative)


def contract(left, right, left_dim, right_dim):
    return lax.dot_general(
        left, right, (((left_dim,), (right_dim,)), ((), ())), preferred_element_type=jnp.float32
    )


def rows_of(value):
    return value.reshape((-1, value.shape[-1]))


def kernel(
    act_hbm, up_hbm, down_hbm, cot_hbm,
    out_hbm, in_grad_hbm, up_grad_hbm, down_grad_hbm,
    tok, w_up, w_down, acc0, s1, r1, acc2, s2, r2, acc3, s3, r3, acc4, s4, r4,
    hp, part, q0, ky, sy, ry, own, ds, rd, up_out, down_out, small_out,
    load_sem, store_sem, send_sem, recv_sem,
):
    bf16, f32 = jnp.bfloat16, jnp.float32
    width = tok.shape[-1]
    half = width // 2
    depth, row, z = lax.axis_index("depth"), lax.axis_index("row"), lax.axis_index("col")
    yl, k = depth // 2, depth % 2
    x, yh = row // 4, row % 4
    f1x, f2x = (x + x // 2) % 2, x // 2
    f1y, f2y = (yh + yh // 2) % 2, yh // 2
    p1x, p2x = {"row": (x + 1 - 2 * (x % 2)) * 4 + yh}, {"row": (3 - x) * 4 + yh}
    p1y, p2y = {"row": x * 4 + yh + 1 - 2 * (yh % 2)}, {"row": x * 4 + 3 - yh}
    sibling, ypartner = {"depth": yl * 2 + 1 - k}, {"depth": (1 - yl) * 2 + k}

    def along(offset):
        return {"col": (z + offset + 8) % 8}

    partners = [sibling, ypartner, p1x, p2x, p1y, p2y] + [along(o) for o in OFFSETS[1:]]

    started = []

    def send(src, dst, device):
        n = len(started)
        copy = pltpu.make_async_remote_copy(
            src_ref=src, dst_ref=dst, send_sem=send_sem.at[n], recv_sem=recv_sem.at[n],
            device_id=device, device_id_type=pl.DeviceIdType.MESH,
        )
        copy.start()
        started.append(copy)
        return copy

    loads = [
        pltpu.make_async_copy(act_hbm, tok.at[0, 0, k, yl], load_sem.at[0]),
        pltpu.make_async_copy(cot_hbm, tok.at[1, 0, k, yl], load_sem.at[1]),
        pltpu.make_async_copy(up_hbm, w_up, load_sem.at[2]),
        pltpu.make_async_copy(down_hbm, w_down, load_sem.at[3]),
    ]
    for load in loads:
        load.start()
    barrier = pltpu.get_barrier_semaphore()
    for device in partners:
        pl.semaphore_signal(barrier, inc=1, device_id=device, device_id_type=pl.DeviceIdType.MESH)
    pl.semaphore_wait(barrier, len(partners))

    flow, across, shared = {}, {}, {}

    def block(slot, a=slice(None)):
        return tok.at[a, slot, k, yl]

    def hop(offset, way, a=slice(None)):
        target = offset - way
        flow[target] = flow.get(target, []) + [
            send(block(slot_of(offset), a), block(slot_of(target), a), along(way))
        ]

    def cross(slot):
        across[slot] = send(block(slot), block(slot), ypartner)

    def arrive(offset):
        for copy in flow[offset]:
            copy.wait_recv()

    def share(slot):
        across[slot].wait_recv()
        mine = tok.at[:, slot, k]
        shared[slot] = send(mine, mine, sibling)

    wave = {}

    def reduce1(c):
        for slot in (2 * c, 2 * c + 1):
            shared[slot].wait_recv()
        for a in range(2):
            i, f = 2 * c + a, (f1x, f2x)[a]
            rows = rows_of(tok[a, 2 * c : 2 * c + 2])
            value = contract(rows, w_up[...], 1, 0) if a == 0 else contract(rows, w_down[...], 1, 1)
            acc0[i] = value.reshape(acc0.shape[1:])
            s1[i] = (acc0[i, 1 - f] if a == 0 else acc0[i, :, 1 - f]).astype(bf16)
            wave[c, a] = send(s1.at[i], r1.at[i], (p1x, p2x)[a])

    def reduce2(c):
        for a in range(2):
            i, f, g = 2 * c + a, (f1x, f2x)[a], (f2x, f1x)[a]
            wave[c, a].wait_recv()

            def total(n):
                kept = acc0[i, f, n] if a == 0 else acc0[i, n, f]
                return kept + r1[i, n].astype(f32)

            value = total(1 - g).astype(bf16)
            s2[i, :, 0] = value[..., :half]
            s2[i, :, 1] = value[..., half:]
            wave[c, a] = send(s2.at[i], r2.at[i], (p2x, p1x)[a])
            value = total(g)
            acc2[i, :, 0] = value[..., :half]
            acc2[i, :, 1] = value[..., half:]

    def reduce3(c):
        for a in range(2):
            i, f = 2 * c + a, (f1y, f2y)[a]
            wave[c, a].wait_recv()

            def total(n):
                if a == 0:
                    return acc2[i, n] + r2[i, n].astype(f32)
                return acc2[i, :, n] + r2[i, :, n].astype(f32)

            s3[i] = total(1 - f).astype(bf16)
            wave[c, a] = send(s3.at[i], r3.at[i], (p1y, p2y)[a])
            acc3[i] = total(f)

    def reduce4(c):
        for a in range(2):
            i, f = 2 * c + a, (f2y, f1y)[a]
            wave[c, a].wait_recv()
            s4[i] = acc3[i, 1 - f] + r3[i, 1 - f].astype(f32)
            wave[c, a] = send(s4.at[i], r4.at[i], (p2y, p1y)[a])
            acc4[i] = acc3[i, f] + r3[i, f].astype(f32)

    def double(c, step):
        for a in range(2):
            if step > 0:
                wave[c, a].wait_recv()
            if step == 0:
                region, device = hp.at[c, a, f1x, f2x, f1y, f2y], (p2y, p1y)[a]
            elif step == 1:
                region = hp.at[c, a, f1x, f2x, f1y] if a == 0 else hp.at[c, a, f1x, f2x, :, f2y]
                device = (p1y, p2y)[a]
            elif step == 2:
                region, device = hp.at[c, a, f1x, f2x], (p2x, p1x)[a]
            else:
                region = hp.at[c, a, f1x] if a == 0 else hp.at[c, a, :, f2x]
                device = (p1x, p2x)[a]
            wave[c, a] = send(region, region, device)

    def activate(c):
        wave[c, 0].wait_recv()
        wave[c, 1].wait_recv()
        activated, derivative = gelu_parts(acc4[2 * c] + r4[2 * c])
        hp[c, 0, f1x, f2x, f1y, f2y] = activated.astype(bf16)
        backed = acc4[2 * c + 1] + r4[2 * c + 1]
        hp[c, 1, f1x, f2x, f1y, f2y] = (backed * derivative).astype(bf16)
        double(c, 0)

    pair, cut, scattered = {}, {}, []

    def project(c):
        for a in range(2):
            wave[c, a].wait_recv()
            low, high = rows_of(hp[c, a, :, :, :, 0]), rows_of(hp[c, a, :, :, :, 1])
            rows = jnp.concatenate([low, high], axis=1)
            value = contract(rows, w_down[...], 1, 0) if a == 0 else contract(rows, w_up[...], 1, 1)
            part[c, a] = value.reshape(part.shape[2:])
            pair[c, a] = send(part.at[c, a, :, 1 - k], q0.at[c, a], sibling)

    def merge(c):
        for a in range(2):
            pair[c, a].wait_recv()
            sy[c, a] = (part[c, a, :, k, 1 - yl] + q0[c, a, :, 1 - yl]).astype(bf16)
        cut[c] = send(sy.at[c], ry.at[c], ypartner)
        for a in range(2):
            ky[c, a] = part[c, a, :, k, yl] + q0[c, a, :, yl]

    def scatter(c):
        cut[c].wait_recv()
        for s in (1, 0):
            slot = 2 * c + s
            value = ky[c, :, s] + ry[c, :, s].astype(f32)
            if slot == 0:
                own[...] = value
            else:
                ds[slot] = value.astype(bf16)
                scattered.append(send(ds.at[slot], rd.at[slot], along(OFFSETS[slot])))

    stores = []

    def store(src, dst):
        stores.append(pltpu.make_async_copy(src, dst, store_sem.at[len(stores)]))
        stores[-1].start()

    def up_grad(h):
        cols = slice(h * half, (h + 1) * half)
        left, right = rows_of(tok[0]), rows_of(hp[:, 1, :, :, :, h])
        up_out[:, cols] = contract(left, right, 0, 0).astype(bf16)
        store(up_out.at[:, cols], up_grad_hbm.at[:, cols])

    def down_grad(h):
        rows = slice(h * half, (h + 1) * half)
        left, right = rows_of(hp[:, 0, :, :, :, h]), rows_of(tok[1])
        down_out[rows, :] = contract(left, right, 0, 0).astype(bf16)
        store(down_out.at[rows], down_grad_hbm.at[rows])

    def begin():
        loads[0].wait()
        loads[1].wait()
        hop(0, 1)
        hop(0, -1)
        cross(0)
        hop(0, 2)
        hop(0, -2)

    def pass_on(offset):
        arrive(offset)
        if offset == 4:
            arrive(-4)
        if offset in (2, -2):
            way = -offset // 2
            hop(offset, way)
            hop(offset, 2 * way, 0 if way == 1 else 1)
        cross(slot_of(offset))

    def grads(n):
        (up_grad, down_grad)[n // 2](n % 2)

    stages = {
        "y": pass_on, "s": share, "r1": reduce1, "r2": reduce2, "r3": reduce3, "r4": reduce4,
        "act": activate, "c1": lambda c: double(c, 1), "c2": lambda c: double(c, 2),
        "c3": lambda c: double(c, 3), "p": project, "m": merge, "z": scatter, "g": grads,
    }
    begin()
    loads[2].wait()
    loads[3].wait()
    for stage, index in ORDER:
        stages[stage](index)
    for copy in scattered:
        copy.wait_recv()
    for a, ref in ((0, out_hbm), (1, in_grad_hbm)):
        total = own[a]
        for slot in range(1, 8):
            total = total + rd[slot, a].astype(f32)
        small_out[a] = total.astype(bf16)
        store(small_out.at[a], ref)
    for copy in started:
        copy.wait_send()
    for copy in stores:
        copy.wait()


COPIES = 128


def place(*refs):
    arrays, results, buffers, load_sem, store_sem = refs[:4], refs[4:8], refs[8:12], refs[12], refs[13]
    loads, stores = [], []
    for src, dst, buffer in zip(arrays, results, buffers):
        rows = src.shape[0]
        step = min(rows, 256)
        for first in range(0, rows, step):
            n, part = len(loads), pl.ds(first, step)
            loads.append(pltpu.make_async_copy(src.at[part], buffer.at[part], load_sem.at[n]))
            stores.append(pltpu.make_async_copy(buffer.at[part], dst.at[part], store_sem.at[n]))
    for load in loads:
        load.start()
    for load, store in zip(loads, stores):
        load.wait()
        store.start()
    for store in stores:
        store.wait()


def shards(activations, weight_up, weight_down, out_grad):
    width, hidden = weight_up.shape
    bf16, f32 = jnp.bfloat16, jnp.float32
    assert activations.shape[0] == BLK and width == hidden

    def vmem(lead, kind):
        return pltpu.VMEM(lead + (BLK, width), kind)

    def halves(lead, kind):
        return pltpu.VMEM(lead + (BLK, hidden // 2), kind)

    pieces = 2 * CHUNKS
    scratch = [
        vmem((2, 8, 2, 2), bf16),
        pltpu.VMEM((width, hidden), bf16), pltpu.VMEM((width, hidden), bf16),
        vmem((pieces, 2, 2, 2), f32), vmem((pieces, 2, 2), bf16), vmem((pieces, 2, 2), bf16),
        halves((pieces, 2, 2), f32), halves((pieces, 2, 2), bf16), halves((pieces, 2, 2), bf16),
        halves((pieces, 2), f32), halves((pieces, 2), bf16), halves((pieces, 2), bf16),
        halves((pieces,), f32), halves((pieces,), f32), halves((pieces,), f32),
        halves((CHUNKS, 2, 2, 2, 2, 2), bf16),
        vmem((CHUNKS, 2, 2, 2, 2), f32), vmem((CHUNKS, 2, 2, 2), f32),
        vmem((CHUNKS, 2, 2), f32), vmem((CHUNKS, 2, 2), bf16), vmem((CHUNKS, 2, 2), bf16),
        vmem((2,), f32), vmem((8, 2), bf16), vmem((8, 2), bf16),
        pltpu.VMEM((width, hidden), bf16), pltpu.VMEM((width, hidden), bf16), vmem((2,), bf16),
        pltpu.SemaphoreType.DMA((4,)), pltpu.SemaphoreType.DMA((6,)),
        pltpu.SemaphoreType.DMA((COPIES,)),
        pltpu.SemaphoreType.DMA((COPIES,)),
    ]
    small = jax.ShapeDtypeStruct(activations.shape, bf16)
    large = jax.ShapeDtypeStruct(weight_up.shape, bf16)
    results = pl.pallas_call(
        kernel,
        out_shape=(small, small, large, large),
        in_specs=[pl.BlockSpec(memory_space=pltpu.HBM)] * 4,
        out_specs=[pl.BlockSpec(memory_space=pltpu.HBM)] * 4,
        scratch_shapes=scratch,
        compiler_params=pltpu.CompilerParams(
            collective_id=0, has_side_effects=True, vmem_limit_bytes=VMEM_MIB * 1024 * 1024
        ),
        cost_estimate=pl.CostEstimate(
            flops=12 * 512 * width * hidden, bytes_accessed=8 * width * hidden, transcendentals=0
        ),
        name="layer",
    )(activations, weight_up, weight_down, out_grad)
    out, in_grad, up_grad, down_grad = results
    up_grad, down_grad, out, in_grad = pl.pallas_call(
        place,
        out_shape=(large, large, small, small),
        in_specs=[pl.BlockSpec(memory_space=pltpu.HBM)] * 4,
        out_specs=[pl.BlockSpec(memory_space=pltpu.HBM)] * 4,
        scratch_shapes=[pltpu.VMEM(result.shape, bf16) for result in (large, large, small, small)]
        + [pltpu.SemaphoreType.DMA((8,)), pltpu.SemaphoreType.DMA((8,))],
        compiler_params=pltpu.CompilerParams(vmem_limit_bytes=VMEM_MIB * 1024 * 1024),
        name="place",
    )(up_grad, down_grad, out, in_grad)
    return out, in_grad, up_grad, down_grad


VMEM_MIB = 60


def solution(mesh):
    placed = (
        P(("depth", "col"), "row"),
        P("row", ("depth", "col")),
        P(("depth", "col"), "row"),
        P(("depth", "col"), "row"),
    )
    return jax.shard_map(
        shards,
        mesh=mesh,
        in_specs=placed,
        out_specs=(
            P(("depth", "col"), "row"),
            P(("depth", "col"), "row"),
            P("row", ("depth", "col")),
            P(("depth", "col"), "row"),
        ),
        check_vma=False,
    )
```

```python
import jax
import jax.numpy as jnp
from jax import lax
from jax.experimental import pallas as pl
from jax.experimental.pallas import tpu as pltpu
from jax.sharding import PartitionSpec as P

tanh_scale = 0.7978845608028654
cubic_coeff = 0.044715

OFFSETS = (0, 1, -1, 2, -2, 3, -3, 4)
CHUNKS = 4
BLK = 16


ORDER = (
    ("t", 0), ("y", 1), ("s", 0), ("y", -1), ("s", 1), ("y", 2),
    ("y", -2), ("s", 2), ("r1", 0, 0), ("r1", 0, 1), ("y", 3), ("s", 3),
    ("y", -3), ("r1", 1, 0), ("s", 4), ("r1", 1, 1), ("s", 5), ("y", 4),
    ("r1", 2, 0), ("s", 6), ("r1", 2, 1), ("r2", 0, 1), ("s", 7), ("r2", 1, 0),
    ("r2", 1, 1), ("r2", 2, 0), ("r1", 3, 1), ("r2", 2, 1), ("r3", 0, 1), ("r1", 3, 0),
    ("r3", 1, 0), ("r3", 1, 1), ("r3", 2, 0), ("r2", 0, 0), ("r3", 2, 1), ("r4", 1, 0),
    ("r4", 1, 1), ("r4", 2, 0), ("r2", 3, 1), ("r4", 2, 1), ("r2", 3, 0), ("r3", 0, 0),
    ("act", 1), ("r3", 3, 1), ("r3", 3, 0), ("act", 2), ("ta", 2), ("c1", 1, 0),
    ("c1", 1, 1), ("r4", 3, 1), ("r4", 3, 0), ("c1", 2, 0), ("r4", 0, 0), ("c2", 1, 0),
    ("r4", 0, 1), ("c1", 2, 1), ("c2", 1, 1), ("act", 3), ("c3", 1, 0), ("c2", 2, 0),
    ("t", 1), ("act", 0), ("c3", 1, 1), ("c2", 2, 1), ("c1", 3, 0), ("c1", 3, 1),
    ("c3", 2, 0), ("p", 1, 0), ("c1", 0, 0), ("c1", 0, 1), ("c2", 3, 0), ("c3", 2, 1),
    ("c2", 3, 1), ("p", 1, 1), ("m", 1, 0), ("c2", 0, 0), ("c3", 3, 0), ("p", 2, 0),
    ("m", 1, 1), ("c2", 0, 1), ("c3", 3, 1), ("p", 2, 1), ("m", 2, 0), ("c3", 0, 0),
    ("z", 1), ("p", 3, 0), ("m", 2, 1), ("p", 3, 1), ("c3", 0, 1), ("m", 3, 0),
    ("z", 2), ("p", 0, 0), ("m", 3, 1), ("ta", 3), ("ta", 1), ("ta", 0),
    ("p", 0, 1), ("z", 3), ("m", 0, 0), ("g", 3), ("m", 0, 1), ("g", 1),
    ("g", 0), ("z", 0), ("g", 2),
)


def slot_of(offset):
    return OFFSETS.index(4 if offset == -4 else offset)


def gelu_parts(preact):
    inner = tanh_scale * (preact + cubic_coeff * preact * preact * preact)
    hyper = jnp.tanh(inner)
    activated = 0.5 * preact * (1.0 + hyper)
    derivative = 0.5 * (1.0 + hyper) + 0.5 * preact * (1.0 - hyper * hyper) * tanh_scale * (
        1.0 + 3.0 * cubic_coeff * preact * preact
    )
    return (activated, derivative)


def contract(left, right, left_dim, right_dim):
    return lax.dot_general(
        left, right, (((left_dim,), (right_dim,)), ((), ())), preferred_element_type=jnp.float32
    )


def rows_of(value):
    return value.reshape((-1, value.shape[-1]))


def kernel(
    act_hbm, up_hbm, down_hbm, cot_hbm,
    out_hbm, in_grad_hbm, up_grad_hbm, down_grad_hbm,
    tok, act_t, w_up, w_down, w_up_t, w_down_t, acc0, s1, r1, acc2, s2, r2, acc3, s3, r3, acc4, s4, r4,
    hp, part, q0, ky, sy, ry, own, ds, rd, up_out, down_out, small_out,
    load_sem, store_sem, send_sem, recv_sem,
):
    bf16, f32 = jnp.bfloat16, jnp.float32
    width = tok.shape[-1]
    half = width // 2
    depth, row, z = lax.axis_index("depth"), lax.axis_index("row"), lax.axis_index("col")
    yl, k = depth // 2, depth % 2
    x, yh = row // 4, row % 4
    f1x, f2x = (x + x // 2) % 2, x // 2
    f1y, f2y = (yh + yh // 2) % 2, yh // 2
    p1x, p2x = {"row": (x + 1 - 2 * (x % 2)) * 4 + yh}, {"row": (3 - x) * 4 + yh}
    p1y, p2y = {"row": x * 4 + yh + 1 - 2 * (yh % 2)}, {"row": x * 4 + 3 - yh}
    sibling, ypartner = {"depth": yl * 2 + 1 - k}, {"depth": (1 - yl) * 2 + k}

    def along(offset):
        return {"col": (z + offset + 8) % 8}

    partners = [sibling, ypartner, p1x, p2x, p1y, p2y] + [along(o) for o in OFFSETS[1:]]

    started = []

    def send(src, dst, device):
        n = len(started)
        copy = pltpu.make_async_remote_copy(
            src_ref=src, dst_ref=dst, send_sem=send_sem.at[n], recv_sem=recv_sem.at[n],
            device_id=device, device_id_type=pl.DeviceIdType.MESH,
        )
        copy.start()
        started.append(copy)
        return copy

    loads = [
        pltpu.make_async_copy(act_hbm, tok.at[0, 0, k, yl], load_sem.at[0]),
        pltpu.make_async_copy(cot_hbm, tok.at[1, 0, k, yl], load_sem.at[1]),
        pltpu.make_async_copy(up_hbm, w_up, load_sem.at[2]),
        pltpu.make_async_copy(down_hbm, w_down, load_sem.at[3]),
    ]
    for load in loads:
        load.start()
    barrier = pltpu.get_barrier_semaphore()
    for device in partners:
        pl.semaphore_signal(barrier, inc=1, device_id=device, device_id_type=pl.DeviceIdType.MESH)
    pl.semaphore_wait(barrier, len(partners))

    flow, across, shared = {}, {}, {}

    def block(slot, a=slice(None)):
        return tok.at[a, slot, k, yl]

    def hop(offset, way, a=slice(None)):
        target = offset - way
        flow[target] = flow.get(target, []) + [
            send(block(slot_of(offset), a), block(slot_of(target), a), along(way))
        ]

    def cross(slot):
        across[slot] = send(block(slot), block(slot), ypartner)

    def arrive(offset):
        for copy in flow[offset]:
            copy.wait_recv()

    def share(slot):
        across[slot].wait_recv()
        mine = tok.at[:, slot, k]
        shared[slot] = send(mine, mine, sibling)

    wave, joined = {}, []

    def flip(which):
        if which == 0:
            w_down_t[...] = w_down[...].T
        else:
            w_up_t[...] = w_up[...].T

    def flip_tokens(c):
        act_t[:, c * 8 * BLK : (c + 1) * 8 * BLK] = rows_of(tok[0, 2 * c : 2 * c + 2]).T

    def reduce1(c, a):
        for slot in (2 * c, 2 * c + 1):
            if slot not in joined:
                shared[slot].wait_recv()
                joined.append(slot)
        i, f = 2 * c + a, (f1x, f2x)[a]
        rows = rows_of(tok[a, 2 * c : 2 * c + 2])
        value = contract(rows, (w_up, w_down_t)[a][...], 1, 0)
        acc0[i] = value.reshape(acc0.shape[1:])
        s1[i] = (acc0[i, 1 - f] if a == 0 else acc0[i, :, 1 - f]).astype(bf16)
        wave[c, a] = send(s1.at[i], r1.at[i], (p1x, p2x)[a])

    def reduce2(c, a):
        i, f, g = 2 * c + a, (f1x, f2x)[a], (f2x, f1x)[a]
        wave[c, a].wait_recv()

        def total(n):
            kept = acc0[i, f, n] if a == 0 else acc0[i, n, f]
            return kept + r1[i, n].astype(f32)

        value = total(1 - g).astype(bf16)
        s2[i, :, 0] = value[..., :half]
        s2[i, :, 1] = value[..., half:]
        wave[c, a] = send(s2.at[i], r2.at[i], (p2x, p1x)[a])
        value = total(g)
        acc2[i, :, 0] = value[..., :half]
        acc2[i, :, 1] = value[..., half:]

    def reduce3(c, a):
        i, f = 2 * c + a, (f1y, f2y)[a]
        wave[c, a].wait_recv()

        def total(n):
            if a == 0:
                return acc2[i, n] + r2[i, n].astype(f32)
            return acc2[i, :, n] + r2[i, :, n].astype(f32)

        s3[i] = total(1 - f).astype(bf16)
        wave[c, a] = send(s3.at[i], r3.at[i], (p1y, p2y)[a])
        acc3[i] = total(f)

    def reduce4(c, a):
        i, f = 2 * c + a, (f2y, f1y)[a]
        wave[c, a].wait_recv()
        s4[i] = acc3[i, 1 - f] + r3[i, 1 - f].astype(f32)
        wave[c, a] = send(s4.at[i], r4.at[i], (p2y, p1y)[a])
        acc4[i] = acc3[i, f] + r3[i, f].astype(f32)

    def double(c, a, step):
        if step > 0:
            wave[c, a].wait_recv()
        if step == 0:
            region, device = hp.at[c, a, f1x, f2x, f1y, f2y], (p2y, p1y)[a]
        elif step == 1:
            region = hp.at[c, a, f1x, f2x, f1y] if a == 0 else hp.at[c, a, f1x, f2x, :, f2y]
            device = (p1y, p2y)[a]
        elif step == 2:
            region, device = hp.at[c, a, f1x, f2x], (p2x, p1x)[a]
        else:
            region = hp.at[c, a, f1x] if a == 0 else hp.at[c, a, :, f2x]
            device = (p1x, p2x)[a]
        wave[c, a] = send(region, region, device)

    def activate(c):
        wave[c, 0].wait_recv()
        wave[c, 1].wait_recv()
        activated, derivative = gelu_parts(acc4[2 * c] + r4[2 * c])
        hp[c, 0, f1x, f2x, f1y, f2y] = activated.astype(bf16)
        double(c, 0, 0)
        backed = acc4[2 * c + 1] + r4[2 * c + 1]
        hp[c, 1, f1x, f2x, f1y, f2y] = (backed * derivative).astype(bf16)
        double(c, 1, 0)

    pair, cut, scattered = {}, {}, []

    def project(c, a):
        wave[c, a].wait_recv()
        low, high = rows_of(hp[c, a, :, :, :, 0]), rows_of(hp[c, a, :, :, :, 1])
        rows = jnp.concatenate([low, high], axis=1)
        value = contract(rows, (w_down, w_up_t)[a][...], 1, 0)
        part[c, a] = value.reshape(part.shape[2:])
        pair[c, a] = send(part.at[c, a, :, 1 - k], q0.at[c, a], sibling)

    def merge(c, a):
        pair[c, a].wait_recv()
        sy[c, a] = (part[c, a, :, k, 1 - yl] + q0[c, a, :, 1 - yl]).astype(bf16)
        cut[c, a] = send(sy.at[c, a], ry.at[c, a], ypartner)
        ky[c, a] = part[c, a, :, k, yl] + q0[c, a, :, yl]

    def scatter(c):
        cut[c, 0].wait_recv()
        cut[c, 1].wait_recv()
        for s in (1, 0):
            slot = 2 * c + s
            value = ky[c, :, s] + ry[c, :, s].astype(f32)
            if slot == 0:
                own[...] = value
            else:
                ds[slot] = value.astype(bf16)
                scattered.append(send(ds.at[slot], rd.at[slot], along(OFFSETS[slot])))

    stores = []

    def store(src, dst):
        stores.append(pltpu.make_async_copy(src, dst, store_sem.at[len(stores)]))
        stores[-1].start()

    def up_grad(h):
        cols = slice(h * half, (h + 1) * half)
        right = rows_of(hp[:, 1, :, :, :, h])
        up_out[:, cols] = contract(act_t[...], right, 1, 0).astype(bf16)
        store(up_out.at[:, cols], up_grad_hbm.at[:, cols])

    def down_grad(h):
        rows = slice(h * half, (h + 1) * half)
        left, right = rows_of(hp[:, 0, :, :, :, h]), rows_of(tok[1])
        down_out[rows, :] = contract(left, right, 0, 0).astype(bf16)
        store(down_out.at[rows], down_grad_hbm.at[rows])

    def begin():
        loads[0].wait()
        loads[1].wait()
        hop(0, 1)
        hop(0, -1)
        cross(0)
        hop(0, 2)
        hop(0, -2)

    def pass_on(offset):
        arrive(offset)
        if offset == 4:
            arrive(-4)
        if offset in (2, -2):
            way = -offset // 2
            hop(offset, way)
            hop(offset, 2 * way, 0 if way == 1 else 1)
        cross(slot_of(offset))

    def grads(n):
        (up_grad, down_grad)[n // 2](n % 2)

    stages = {
        "y": pass_on, "s": share, "t": flip, "ta": flip_tokens, "r1": reduce1, "r2": reduce2,
        "r3": reduce3, "r4": reduce4, "act": activate, "c1": lambda c, a: double(c, a, 1),
        "c2": lambda c, a: double(c, a, 2), "c3": lambda c, a: double(c, a, 3),
        "p": project, "m": merge, "z": scatter, "g": grads,
    }
    begin()
    loads[2].wait()
    loads[3].wait()
    for stage, *where in ORDER:
        stages[stage](*where)
    for copy in scattered:
        copy.wait_recv()
    for a, ref in ((0, out_hbm), (1, in_grad_hbm)):
        total = own[a]
        for slot in range(1, 8):
            total = total + rd[slot, a].astype(f32)
        small_out[a] = total.astype(bf16)
        store(small_out.at[a], ref)
    for copy in started:
        copy.wait_send()
    for copy in stores:
        copy.wait()


COPIES = 128


def place(*refs):
    arrays, results, buffers, load_sem, store_sem = refs[:4], refs[4:8], refs[8:12], refs[12], refs[13]
    loads, stores = [], []
    for src, dst, buffer in zip(arrays, results, buffers):
        rows = src.shape[0]
        step = min(rows, 256)
        for first in range(0, rows, step):
            n, part = len(loads), pl.ds(first, step)
            loads.append(pltpu.make_async_copy(src.at[part], buffer.at[part], load_sem.at[n]))
            stores.append(pltpu.make_async_copy(buffer.at[part], dst.at[part], store_sem.at[n]))
    for load in loads:
        load.start()
    for load, store in zip(loads, stores):
        load.wait()
        store.start()
    for store in stores:
        store.wait()


def shards(activations, weight_up, weight_down, out_grad):
    width, hidden = weight_up.shape
    bf16, f32 = jnp.bfloat16, jnp.float32
    assert activations.shape[0] == BLK and width == hidden

    def vmem(lead, kind):
        return pltpu.VMEM(lead + (BLK, width), kind)

    def halves(lead, kind):
        return pltpu.VMEM(lead + (BLK, hidden // 2), kind)

    pieces = 2 * CHUNKS
    scratch = [
        vmem((2, 8, 2, 2), bf16),
        pltpu.VMEM((width, 8 * CHUNKS * BLK), bf16),
        pltpu.VMEM((width, hidden), bf16), pltpu.VMEM((width, hidden), bf16),
        pltpu.VMEM((width, hidden), bf16), pltpu.VMEM((width, hidden), bf16),
        vmem((pieces, 2, 2, 2), f32), vmem((pieces, 2, 2), bf16), vmem((pieces, 2, 2), bf16),
        halves((pieces, 2, 2), f32), halves((pieces, 2, 2), bf16), halves((pieces, 2, 2), bf16),
        halves((pieces, 2), f32), halves((pieces, 2), bf16), halves((pieces, 2), bf16),
        halves((pieces,), f32), halves((pieces,), f32), halves((pieces,), f32),
        halves((CHUNKS, 2, 2, 2, 2, 2), bf16),
        vmem((CHUNKS, 2, 2, 2, 2), f32), vmem((CHUNKS, 2, 2, 2), f32),
        vmem((CHUNKS, 2, 2), f32), vmem((CHUNKS, 2, 2), bf16), vmem((CHUNKS, 2, 2), bf16),
        vmem((2,), f32), vmem((8, 2), bf16), vmem((8, 2), bf16),
        pltpu.VMEM((width, hidden), bf16), pltpu.VMEM((width, hidden), bf16), vmem((2,), bf16),
        pltpu.SemaphoreType.DMA((4,)), pltpu.SemaphoreType.DMA((6,)),
        pltpu.SemaphoreType.DMA((COPIES,)),
        pltpu.SemaphoreType.DMA((COPIES,)),
    ]
    small = jax.ShapeDtypeStruct(activations.shape, bf16)
    large = jax.ShapeDtypeStruct(weight_up.shape, bf16)
    results = pl.pallas_call(
        kernel,
        out_shape=(small, small, large, large),
        in_specs=[pl.BlockSpec(memory_space=pltpu.HBM)] * 4,
        out_specs=[pl.BlockSpec(memory_space=pltpu.HBM)] * 4,
        scratch_shapes=scratch,
        compiler_params=pltpu.CompilerParams(
            collective_id=0, has_side_effects=True, vmem_limit_bytes=VMEM_MIB * 1024 * 1024
        ),
        cost_estimate=pl.CostEstimate(
            flops=12 * 512 * width * hidden, bytes_accessed=8 * width * hidden, transcendentals=0
        ),
        name="layer",
    )(activations, weight_up, weight_down, out_grad)
    out, in_grad, up_grad, down_grad = results
    up_grad, down_grad, out, in_grad = pl.pallas_call(
        place,
        out_shape=(large, large, small, small),
        in_specs=[pl.BlockSpec(memory_space=pltpu.HBM)] * 4,
        out_specs=[pl.BlockSpec(memory_space=pltpu.HBM)] * 4,
        scratch_shapes=[pltpu.VMEM(result.shape, bf16) for result in (large, large, small, small)]
        + [pltpu.SemaphoreType.DMA((8,)), pltpu.SemaphoreType.DMA((8,))],
        compiler_params=pltpu.CompilerParams(vmem_limit_bytes=VMEM_MIB * 1024 * 1024),
        name="place",
    )(up_grad, down_grad, out, in_grad)
    return out, in_grad, up_grad, down_grad


VMEM_MIB = 60


def solution(mesh):
    placed = (
        P(("depth", "col"), "row"),
        P("row", ("depth", "col")),
        P(("depth", "col"), "row"),
        P(("depth", "col"), "row"),
    )
    return jax.shard_map(
        shards,
        mesh=mesh,
        in_specs=placed,
        out_specs=(
            P(("depth", "col"), "row"),
            P(("depth", "col"), "row"),
            P("row", ("depth", "col")),
            P(("depth", "col"), "row"),
        ),
        check_vma=False,
    )
```

```python
import jax
import jax.numpy as jnp
from jax import lax
from jax.experimental import pallas as pl
from jax.experimental.pallas import tpu as pltpu
from jax.sharding import PartitionSpec as P

tanh_scale = 0.7978845608028654
cubic_coeff = 0.044715

OFFSETS = (0, 1, -1, 2, -2, 3, -3, 4)
CHUNKS = 4
BLK = 16


ORDER = (
    ("y", 1), ("y", -1), ("y", 2), ("s", 0), ("y", -2), ("y", 3),
    ("s", 1), ("r1", 0, 0), ("r1", 0, 1), ("y", -3), ("y", 4), ("r1", 1, 0),
    ("r1", 1, 1), ("s", 2), ("r2", 0, 0), ("s", 3), ("r2", 0, 1), ("r2", 1, 0),
    ("r2", 1, 1), ("r1", 3, 1), ("r1", 3, 0), ("r1", 2, 0), ("r3", 1), ("r3", 0),
    ("r1", 2, 1), ("r2", 3, 0), ("r2", 3, 1), ("r4", 1), ("r4", 0), ("r2", 2, 0),
    ("r2", 2, 1), ("r3", 3), ("act", 1), ("r3", 2), ("act", 0), ("c1", 1),
    ("ta", 0), ("r4", 3), ("r4", 2), ("c1", 0), ("c2", 1, 1), ("c2", 1, 0),
    ("ta", 1), ("act", 3), ("act", 2), ("c3", 1, 0), ("c2", 0, 0), ("c1", 3),
    ("c3", 1, 1), ("c1", 2), ("ta", 3), ("c2", 0, 1), ("c3", 0, 0), ("c2", 3, 0),
    ("ta", 2), ("c2", 2, 0), ("c2", 2, 1), ("c3", 0, 1), ("c2", 3, 1), ("p", 1),
    ("c3", 2, 1), ("c3", 2, 0), ("c3", 3, 0), ("c3", 3, 1), ("p", 0), ("m", 1),
    ("p", 2), ("m", 0), ("p", 3), ("m", 2), ("z", 1), ("z", 0),
    ("m", 3), ("z", 2), ("z", 3), ("g", 3), ("g", 2), ("g", 1),
    ("g", 0),
)


def slot_of(offset):
    return OFFSETS.index(4 if offset == -4 else offset)


def gelu_parts(preact):
    inner = tanh_scale * (preact + cubic_coeff * preact * preact * preact)
    hyper = jnp.tanh(inner)
    activated = 0.5 * preact * (1.0 + hyper)
    derivative = 0.5 * (1.0 + hyper) + 0.5 * preact * (1.0 - hyper * hyper) * tanh_scale * (
        1.0 + 3.0 * cubic_coeff * preact * preact
    )
    return (activated, derivative)


def contract(left, right, left_dim, right_dim):
    return lax.dot_general(
        left, right, (((left_dim,), (right_dim,)), ((), ())), preferred_element_type=jnp.float32
    )


def rows_of(value):
    return value.reshape((-1, value.shape[-1]))


def kernel(
    act_hbm, up_hbm, down_hbm, cot_hbm,
    out_hbm, in_grad_hbm, up_grad_hbm, down_grad_hbm,
    tok, act_t, w_up, w_down, acc0, s1, r1, acc2, s2, r2, acc3, s3, r3, acc4, s4, r4,
    hp, part, q0, ky, sy, ry, own, ds, rd, up_out, down_out, small_out,
    load_sem, store_sem, send_sem, recv_sem,
):
    bf16, f32 = jnp.bfloat16, jnp.float32
    width = tok.shape[-1]
    half = width // 2
    depth, row, z = lax.axis_index("depth"), lax.axis_index("row"), lax.axis_index("col")
    yl, k = depth // 2, depth % 2
    x, yh = row // 4, row % 4
    f1x, f2x = (x + x // 2) % 2, x // 2
    f1y, f2y = (yh + yh // 2) % 2, yh // 2
    def device(depth_at, row_at, col_at):
        return {"depth": depth_at, "row": row_at, "col": col_at}

    p1x = device(depth, (x + 1 - 2 * (x % 2)) * 4 + yh, z)
    p2x = device(depth, (3 - x) * 4 + yh, z)
    p1y = device(depth, x * 4 + yh + 1 - 2 * (yh % 2), z)
    p2y = device(depth, x * 4 + 3 - yh, z)
    sibling = device(yl * 2 + 1 - k, row, z)
    ypartner = device((1 - yl) * 2 + k, row, z)
    cols = {offset: device(depth, row, (z + offset + 8) % 8) for offset in OFFSETS[1:]}

    def along(offset):
        return cols[offset]

    partners = [sibling, ypartner, p1x, p2x, p1y, p2y] + [along(o) for o in OFFSETS[1:]]

    started, kinds = [], []

    def send(kind, src, dst, target):
        n = len(started)
        if kind not in kinds:
            kinds.append(kind)
        copy = pltpu.make_async_remote_copy(
            src_ref=src, dst_ref=dst, send_sem=send_sem.at[kinds.index(kind)],
            recv_sem=recv_sem.at[n], device_id=target,
            device_id_type=pl.DeviceIdType.MESH,
        )
        copy.start()
        started.append(copy)
        return copy

    loads = [
        pltpu.make_async_copy(act_hbm, tok.at[0, k, 0, yl], load_sem.at[0]),
        pltpu.make_async_copy(cot_hbm, tok.at[0, k, 1, yl], load_sem.at[1]),
        pltpu.make_async_copy(up_hbm, w_up, load_sem.at[2]),
        pltpu.make_async_copy(down_hbm, w_down, load_sem.at[3]),
    ]
    for load in loads:
        load.start()
    barrier = pltpu.get_barrier_semaphore()
    for target in partners:
        pl.semaphore_signal(
            barrier, inc=1, device_id=target, device_id_type=pl.DeviceIdType.MESH
        )
    pl.semaphore_wait(barrier, len(partners))

    flow, across, shared = {}, {}, {}

    def block(slot, a=slice(None)):
        return tok.at[slot, k, a, yl]

    def hop(offset, way, a=slice(None)):
        target = offset - way
        flow[target] = flow.get(target, []) + [
            send("hop", block(slot_of(offset), a), block(slot_of(target), a), along(way))
        ]

    def cross(slot):
        across[slot] = send("cross", block(slot), block(slot), ypartner)

    def arrive(offset):
        for copy in flow[offset]:
            copy.wait_recv()

    def share(c):
        for slot in (2 * c, 2 * c + 1):
            across[slot].wait_recv()
        mine = tok.at[2 * c : 2 * c + 2, k]
        shared[c] = send("share", mine, mine, sibling)

    wave, joined, widened = {}, [], []

    def flip_tokens(c):
        act_t[:, c * 8 * BLK : (c + 1) * 8 * BLK] = rows_of(tok[2 * c : 2 * c + 2, :, 0]).T

    def reduce1(c, a):
        if c not in joined:
            shared[c].wait_recv()
            joined.append(c)
        i, f = 2 * c + a, (f1x, f2x)[a]
        rows = rows_of(tok[2 * c : 2 * c + 2, :, a])
        value = contract(rows, (w_up, w_down)[a][...], 1, a)
        acc0[i] = value.reshape(acc0.shape[1:])
        s1[i] = (acc0[i, 1 - f] if a == 0 else acc0[i, :, 1 - f]).astype(bf16)
        wave[c, a] = send("s1", s1.at[i], r1.at[i], (p1x, p2x)[a])

    def reduce2(c, a):
        i, f, g = 2 * c + a, (f1x, f2x)[a], (f2x, f1x)[a]
        wave[c, a].wait_recv()

        def total(n):
            kept = acc0[i, f, n] if a == 0 else acc0[i, n, f]
            return kept + r1[i, n].astype(f32)

        value = total(1 - g).astype(bf16)
        s2[i, :, 0] = value[..., :half]
        s2[i, :, 1] = value[..., half:]
        wave[c, a] = send("s2", s2.at[i], r2.at[i], (p2x, p1x)[a])
        value = total(g)
        acc2[i, :, 0] = value[..., :half]
        acc2[i, :, 1] = value[..., half:]

    def reduce3(c):
        pair_of, f = slice(2 * c, 2 * c + 2), (f1y, f2y)[c % 2]
        wave[c, 0].wait_recv()
        wave[c, 1].wait_recv()

        def total(n):
            if c % 2 == 0:
                return acc2[pair_of, n] + r2[pair_of, n].astype(f32)
            return acc2[pair_of, :, n] + r2[pair_of, :, n].astype(f32)

        s3[pair_of] = total(1 - f).astype(bf16)
        wave[c] = send("s3", s3.at[pair_of], r3.at[pair_of], (p1y, p2y)[c % 2])
        acc3[pair_of] = total(f)

    def reduce4(c):
        pair_of, f = slice(2 * c, 2 * c + 2), (f2y, f1y)[c % 2]
        wave[c].wait_recv()
        s4[pair_of] = acc3[pair_of, 1 - f] + r3[pair_of, 1 - f].astype(f32)
        wave[c] = send("s4", s4.at[pair_of], r4.at[pair_of], (p2y, p1y)[c % 2])
        acc4[pair_of] = acc3[pair_of, f] + r3[pair_of, f].astype(f32)

    def activate(c):
        wave[c].wait_recv()
        activated, derivative = gelu_parts(acc4[2 * c] + r4[2 * c])
        backed = acc4[2 * c + 1] + r4[2 * c + 1]
        hp[c, 0, f1x, f2x, f1y, f2y] = activated.astype(bf16)
        hp[c, 1, f1x, f2x, f1y, f2y] = (backed * derivative).astype(bf16)
        region = hp.at[c, :, f1x, f2x, f1y, f2y]
        wave[c] = send("d0", region, region, (p2y, p1y)[c % 2])

    def double1(c):
        wave[c].wait_recv()
        region = hp.at[c, :, f1x, f2x, f1y] if c % 2 == 0 else hp.at[c, :, f1x, f2x, :, f2y]
        wave[c] = send("d1", region, region, (p1y, p2y)[c % 2])

    def double2(c, a):
        if c not in widened:
            wave[c].wait_recv()
            widened.append(c)
        region = hp.at[c, a, f1x, f2x]
        wave[c, a] = send("d2", region, region, (p2x, p1x)[a])

    def double3(c, a):
        wave[c, a].wait_recv()
        region = hp.at[c, a, f1x] if a == 0 else hp.at[c, a, :, f2x]
        wave[c, a] = send("d3", region, region, (p1x, p2x)[a])

    pair, cut, scattered = {}, {}, []

    def project(c):
        for a in range(2):
            wave[c, a].wait_recv()
            low, high = rows_of(hp[c, a, :, :, :, 0]), rows_of(hp[c, a, :, :, :, 1])
            rows = jnp.concatenate([low, high], axis=1)
            value = contract(rows, (w_down, w_up)[a][...], 1, a).reshape((2, 2, 2, BLK, width))
            part[c, 0, a] = value[:, 0]
            part[c, 1, a] = value[:, 1]
        pair[c] = send("part", part.at[c, 1 - k], q0.at[c], sibling)

    def merge(c):
        pair[c].wait_recv()
        sy[c] = (part[c, k, :, :, 1 - yl] + q0[c, :, :, 1 - yl]).astype(bf16)
        cut[c] = send("sy", sy.at[c], ry.at[c], ypartner)
        ky[c] = part[c, k, :, :, yl] + q0[c, :, :, yl]

    def scatter(c):
        cut[c].wait_recv()
        for s in (1, 0):
            slot = 2 * c + s
            value = ky[c, :, s] + ry[c, :, s].astype(f32)
            if slot == 0:
                own[...] = value
            else:
                ds[slot] = value.astype(bf16)
                scattered.append(send("ds", ds.at[slot], rd.at[slot], along(OFFSETS[slot])))

    stores = []

    def store(src, dst):
        stores.append(pltpu.make_async_copy(src, dst, store_sem.at[len(stores)]))
        stores[-1].start()

    def up_grad(h):
        cols = slice(h * half, (h + 1) * half)
        right = rows_of(hp[:, 1, :, :, :, h])
        up_out[:, cols] = contract(act_t[...], right, 1, 0).astype(bf16)
        store(up_out.at[:, cols], up_grad_hbm.at[:, cols])

    def down_grad(h):
        rows = slice(h * half, (h + 1) * half)
        left, right = rows_of(hp[:, 0, :, :, :, h]), rows_of(tok[:, :, 1])
        down_out[rows, :] = contract(left, right, 0, 0).astype(bf16)
        store(down_out.at[rows], down_grad_hbm.at[rows])

    def begin():
        loads[0].wait()
        loads[1].wait()
        hop(0, 1)
        hop(0, -1)
        cross(0)
        hop(0, 2)
        hop(0, -2)

    def pass_on(offset):
        arrive(offset)
        if offset == 4:
            arrive(-4)
        if offset in (2, -2):
            way = -offset // 2
            hop(offset, way)
            hop(offset, 2 * way, 0 if way == 1 else 1)
        cross(slot_of(offset))

    def grads(n):
        (up_grad, down_grad)[n // 2](n % 2)

    stages = {
        "y": pass_on, "s": share, "ta": flip_tokens, "r1": reduce1, "r2": reduce2,
        "r3": reduce3, "r4": reduce4, "act": activate, "c1": double1, "c2": double2,
        "c3": double3, "p": project, "m": merge, "z": scatter, "g": grads,
    }
    begin()
    loads[2].wait()
    loads[3].wait()
    for stage, *where in ORDER:
        stages[stage](*where)
    for copy in scattered:
        copy.wait_recv()
    for a, ref in ((0, out_hbm), (1, in_grad_hbm)):
        total = own[a]
        for slot in range(1, 8):
            total = total + rd[slot, a].astype(f32)
        small_out[a] = total.astype(bf16)
        store(small_out.at[a], ref)
    sent = {
        "hop": tok.at[0:7, 0, :, 0], "cross": tok.at[:, 0, :, 0], "share": tok.at[:, 0],
        "s1": s1, "s2": s2, "s3": s3, "s4": s4, "d0": hp.at[:, :, 0, 0, 0, 0],
        "d1": hp.at[:, :, 0, 0, 0], "d2": hp.at[:, :, 0, 0], "d3": hp.at[:, :, 0],
        "part": q0, "sy": sy, "ds": ds.at[1:8],
    }
    for kind, ref in sent.items():
        pltpu.make_async_copy(ref, ref, send_sem.at[kinds.index(kind)]).wait()
    for copy in stores:
        copy.wait()


KINDS, COPIES = 14, 96


def place(*refs):
    arrays, results, buffers, load_sem, store_sem = refs[:4], refs[4:8], refs[8:12], refs[12], refs[13]
    loads, stores = [], []
    for src, dst, buffer in zip(arrays, results, buffers):
        rows = src.shape[0]
        step = min(rows, 256)
        for first in range(0, rows, step):
            n, part = len(loads), pl.ds(first, step)
            loads.append(pltpu.make_async_copy(src.at[part], buffer.at[part], load_sem.at[n]))
            stores.append(pltpu.make_async_copy(buffer.at[part], dst.at[part], store_sem.at[n]))
    for load in loads:
        load.start()
    for load, store in zip(loads, stores):
        load.wait()
        store.start()
    for store in stores:
        store.wait()


def shards(activations, weight_up, weight_down, out_grad):
    width, hidden = weight_up.shape
    bf16, f32 = jnp.bfloat16, jnp.float32
    assert activations.shape[0] == BLK and width == hidden

    def vmem(lead, kind):
        return pltpu.VMEM(lead + (BLK, width), kind)

    def halves(lead, kind):
        return pltpu.VMEM(lead + (BLK, hidden // 2), kind)

    pieces = 2 * CHUNKS
    scratch = [
        vmem((8, 2, 2, 2), bf16),
        pltpu.VMEM((width, 8 * CHUNKS * BLK), bf16),
        pltpu.VMEM((width, hidden), bf16), pltpu.VMEM((width, hidden), bf16),
        vmem((pieces, 2, 2, 2), f32), vmem((pieces, 2, 2), bf16), vmem((pieces, 2, 2), bf16),
        halves((pieces, 2, 2), f32), halves((pieces, 2, 2), bf16), halves((pieces, 2, 2), bf16),
        halves((pieces, 2), f32), halves((pieces, 2), bf16), halves((pieces, 2), bf16),
        halves((pieces,), f32), halves((pieces,), f32), halves((pieces,), f32),
        halves((CHUNKS, 2, 2, 2, 2, 2), bf16),
        vmem((CHUNKS, 2, 2, 2, 2), f32), vmem((CHUNKS, 2, 2, 2), f32),
        vmem((CHUNKS, 2, 2), f32), vmem((CHUNKS, 2, 2), bf16), vmem((CHUNKS, 2, 2), bf16),
        vmem((2,), f32), vmem((8, 2), bf16), vmem((8, 2), bf16),
        pltpu.VMEM((width, hidden), bf16), pltpu.VMEM((width, hidden), bf16), vmem((2,), bf16),
        pltpu.SemaphoreType.DMA((4,)), pltpu.SemaphoreType.DMA((6,)),
        pltpu.SemaphoreType.DMA((KINDS,)), pltpu.SemaphoreType.DMA((COPIES,)),
    ]
    small = jax.ShapeDtypeStruct(activations.shape, bf16)
    large = jax.ShapeDtypeStruct(weight_up.shape, bf16)
    results = pl.pallas_call(
        kernel,
        out_shape=(small, small, large, large),
        in_specs=[pl.BlockSpec(memory_space=pltpu.HBM)] * 4,
        out_specs=[pl.BlockSpec(memory_space=pltpu.HBM)] * 4,
        scratch_shapes=scratch,
        compiler_params=pltpu.CompilerParams(
            collective_id=0, has_side_effects=True, vmem_limit_bytes=VMEM_MIB * 1024 * 1024
        ),
        cost_estimate=pl.CostEstimate(
            flops=12 * 512 * width * hidden, bytes_accessed=8 * width * hidden, transcendentals=0
        ),
        name="layer",
    )(activations, weight_up, weight_down, out_grad)
    out, in_grad, up_grad, down_grad = results
    up_grad, down_grad, out, in_grad = pl.pallas_call(
        place,
        out_shape=(large, large, small, small),
        in_specs=[pl.BlockSpec(memory_space=pltpu.HBM)] * 4,
        out_specs=[pl.BlockSpec(memory_space=pltpu.HBM)] * 4,
        scratch_shapes=[pltpu.VMEM(result.shape, bf16) for result in (large, large, small, small)]
        + [pltpu.SemaphoreType.DMA((8,)), pltpu.SemaphoreType.DMA((8,))],
        compiler_params=pltpu.CompilerParams(vmem_limit_bytes=VMEM_MIB * 1024 * 1024),
        name="place",
    )(up_grad, down_grad, out, in_grad)
    return out, in_grad, up_grad, down_grad


VMEM_MIB = 60


def solution(mesh):
    placed = (
        P(("depth", "col"), "row"),
        P("row", ("depth", "col")),
        P(("depth", "col"), "row"),
        P(("depth", "col"), "row"),
    )
    return jax.shard_map(
        shards,
        mesh=mesh,
        in_specs=placed,
        out_specs=(
            P(("depth", "col"), "row"),
            P(("depth", "col"), "row"),
            P("row", ("depth", "col")),
            P(("depth", "col"), "row"),
        ),
        check_vma=False,
    )
```

```python
import jax
import jax.numpy as jnp
from jax import lax
from jax.experimental import pallas as pl
from jax.experimental.pallas import tpu as pltpu
from jax.sharding import PartitionSpec as P

tanh_scale = 0.7978845608028654
cubic_coeff = 0.044715

OFFSETS = (0, 1, -1, 2, -2, 3, -3, 4)
CHUNKS = 4
Y_FIRST = (2,)
BLK = 16


ORDER = (
    ("t", 0), ("y", 1), ("s", 0), ("y", -1), ("s", 1), ("y", 2),
    ("y", -2), ("s", 2), ("r1", 0, 0), ("r1", 0, 1), ("y", 3), ("s", 3),
    ("y", -3), ("r1", 1, 0), ("s", 4), ("r1", 1, 1), ("s", 5), ("y", 4),
    ("r1", 2, 0), ("s", 6), ("r1", 2, 1), ("r2", 0, 1), ("s", 7), ("r2", 1, 0),
    ("r2", 1, 1), ("r2", 2, 0), ("r1", 3, 1), ("r2", 2, 1), ("r3", 0, 1), ("r1", 3, 0),
    ("r3", 1, 0), ("r3", 1, 1), ("r3", 2, 0), ("r2", 0, 0), ("r3", 2, 1), ("r4", 1, 0),
    ("r4", 1, 1), ("r4", 2, 0), ("r2", 3, 1), ("r4", 2, 1), ("r2", 3, 0), ("r3", 0, 0),
    ("act", 1), ("r3", 3, 1), ("r3", 3, 0), ("act", 2), ("ta", 2), ("c1", 1, 0),
    ("c1", 1, 1), ("r4", 3, 1), ("r4", 3, 0), ("c1", 2, 0), ("r4", 0, 0), ("c2", 1, 0),
    ("r4", 0, 1), ("c1", 2, 1), ("c2", 1, 1), ("act", 3), ("c3", 1, 0), ("c2", 2, 0),
    ("t", 1), ("act", 0), ("c3", 1, 1), ("c2", 2, 1), ("c1", 3, 0), ("c1", 3, 1),
    ("c3", 2, 0), ("p", 1, 0), ("c1", 0, 0), ("c1", 0, 1), ("c2", 3, 0), ("c3", 2, 1),
    ("c2", 3, 1), ("p", 1, 1), ("m", 1, 0), ("c2", 0, 0), ("c3", 3, 0), ("p", 2, 0),
    ("m", 1, 1), ("c2", 0, 1), ("c3", 3, 1), ("p", 2, 1), ("m", 2, 0), ("c3", 0, 0),
    ("z", 1), ("p", 3, 0), ("m", 2, 1), ("p", 3, 1), ("c3", 0, 1), ("m", 3, 0),
    ("z", 2), ("p", 0, 0), ("m", 3, 1), ("ta", 3), ("ta", 1), ("ta", 0),
    ("p", 0, 1), ("z", 3), ("m", 0, 0), ("g", 3), ("m", 0, 1), ("g", 1),
    ("g", 0), ("z", 0), ("g", 2),
)


def slot_of(offset):
    return OFFSETS.index(4 if offset == -4 else offset)


def gelu_parts(preact):
    inner = tanh_scale * (preact + cubic_coeff * preact * preact * preact)
    hyper = jnp.tanh(inner)
    activated = 0.5 * preact * (1.0 + hyper)
    derivative = 0.5 * (1.0 + hyper) + 0.5 * preact * (1.0 - hyper * hyper) * tanh_scale * (
        1.0 + 3.0 * cubic_coeff * preact * preact
    )
    return (activated, derivative)


def contract(left, right, left_dim, right_dim):
    return lax.dot_general(
        left, right, (((left_dim,), (right_dim,)), ((), ())), preferred_element_type=jnp.float32
    )


def rows_of(value):
    return value.reshape((-1, value.shape[-1]))


def kernel(
    act_hbm, up_hbm, down_hbm, cot_hbm,
    out_hbm, in_grad_hbm, up_grad_hbm, down_grad_hbm,
    tok, act_t, w_up, w_down, w_up_t, w_down_t, acc0, s1, r1, acc2, s2, r2, acc3, s3, r3, acc4, s4, r4,
    hp, part, q0, ky, sy, ry, own, ds, rd, up_out, down_out, small_out,
    load_sem, store_sem, send_sem, recv_sem,
):
    bf16, f32 = jnp.bfloat16, jnp.float32
    width = tok.shape[-1]
    half = width // 2
    depth, row, z = lax.axis_index("depth"), lax.axis_index("row"), lax.axis_index("col")
    yl, k = depth // 2, depth % 2
    x, yh = row // 4, row % 4
    f1x, f2x = (x + x // 2) % 2, x // 2
    f1y, f2y = (yh + yh // 2) % 2, yh // 2
    p1x, p2x = {"row": (x + 1 - 2 * (x % 2)) * 4 + yh}, {"row": (3 - x) * 4 + yh}
    p1y, p2y = {"row": x * 4 + yh + 1 - 2 * (yh % 2)}, {"row": x * 4 + 3 - yh}
    sibling, ypartner = {"depth": yl * 2 + 1 - k}, {"depth": (1 - yl) * 2 + k}

    def along(offset):
        return {"col": (z + offset + 8) % 8}

    x_first = (f1x, f2x, f1y, f2y), (p1x, p2x, p1y, p2y)
    y_first = (f1y, f2y, f1x, f2x), (p1y, p2y, p1x, p2x)

    def roles(c):
        return y_first if c in Y_FIRST else x_first

    partners = [sibling, ypartner, p1x, p2x, p1y, p2y] + [along(o) for o in OFFSETS[1:]]

    started, kinds = [], []

    def send(kind, src, dst, device):
        n = len(started)
        if kind not in kinds:
            kinds.append(kind)
        copy = pltpu.make_async_remote_copy(
            src_ref=src, dst_ref=dst, send_sem=send_sem.at[kinds.index(kind)],
            recv_sem=recv_sem.at[n],
            device_id=device, device_id_type=pl.DeviceIdType.MESH,
        )
        copy.start()
        started.append(copy)
        return copy

    loads = [
        pltpu.make_async_copy(act_hbm, tok.at[0, 0, k, yl], load_sem.at[0]),
        pltpu.make_async_copy(cot_hbm, tok.at[1, 0, k, yl], load_sem.at[1]),
        pltpu.make_async_copy(up_hbm, w_up, load_sem.at[2]),
        pltpu.make_async_copy(down_hbm, w_down, load_sem.at[3]),
    ]
    for load in loads:
        load.start()
    barrier = pltpu.get_barrier_semaphore()
    for device in partners:
        pl.semaphore_signal(barrier, inc=1, device_id=device, device_id_type=pl.DeviceIdType.MESH)
    pl.semaphore_wait(barrier, len(partners))

    flow, across, shared = {}, {}, {}

    def block(slot, a=slice(None)):
        return tok.at[a, slot, k, yl]

    def hop(offset, way, a=slice(None)):
        target = offset - way
        flow[target] = flow.get(target, []) + [
            send("hop", block(slot_of(offset), a), block(slot_of(target), a), along(way))
        ]

    def cross(slot):
        across[slot] = send("cross", block(slot), block(slot), ypartner)

    def arrive(offset):
        for copy in flow[offset]:
            copy.wait_recv()

    def share(slot):
        across[slot].wait_recv()
        mine = tok.at[:, slot, k]
        shared[slot] = send("share", mine, mine, sibling)

    wave, joined = {}, []

    def flip(which):
        if which == 0:
            w_down_t[...] = w_down[...].T
        else:
            w_up_t[...] = w_up[...].T

    def flip_tokens(c):
        act_t[:, c * 8 * BLK : (c + 1) * 8 * BLK] = rows_of(tok[0, 2 * c : 2 * c + 2]).T

    def reduce1(c, a):
        for slot in (2 * c, 2 * c + 1):
            if slot not in joined:
                shared[slot].wait_recv()
                joined.append(slot)
        (b1, b2, _, _), (p1, p2, _, _) = roles(c)
        i, f = 2 * c + a, (b1, b2)[a]
        rows = rows_of(tok[a, 2 * c : 2 * c + 2])
        value = contract(rows, (w_up, w_down_t)[a][...], 1, 0)
        acc0[i] = value.reshape(acc0.shape[1:])
        s1[i] = (acc0[i, 1 - f] if a == 0 else acc0[i, :, 1 - f]).astype(bf16)
        wave[c, a] = send("s1", s1.at[i], r1.at[i], (p1, p2)[a])

    def reduce2(c, a):
        (b1, b2, _, _), (p1, p2, _, _) = roles(c)
        i, f, g = 2 * c + a, (b1, b2)[a], (b2, b1)[a]
        wave[c, a].wait_recv()

        def total(n):
            kept = acc0[i, f, n] if a == 0 else acc0[i, n, f]
            return kept + r1[i, n].astype(f32)

        value = total(1 - g).astype(bf16)
        s2[i, :, 0] = value[..., :half]
        s2[i, :, 1] = value[..., half:]
        wave[c, a] = send("s2", s2.at[i], r2.at[i], (p2, p1)[a])
        value = total(g)
        acc2[i, :, 0] = value[..., :half]
        acc2[i, :, 1] = value[..., half:]

    def reduce3(c, a):
        (_, _, b3, b4), (_, _, p3, p4) = roles(c)
        i, f = 2 * c + a, (b3, b4)[a]
        wave[c, a].wait_recv()

        def total(n):
            if a == 0:
                return acc2[i, n] + r2[i, n].astype(f32)
            return acc2[i, :, n] + r2[i, :, n].astype(f32)

        s3[i] = total(1 - f).astype(bf16)
        wave[c, a] = send("s3", s3.at[i], r3.at[i], (p3, p4)[a])
        acc3[i] = total(f)

    def reduce4(c, a):
        (_, _, b3, b4), (_, _, p3, p4) = roles(c)
        i, f = 2 * c + a, (b4, b3)[a]
        wave[c, a].wait_recv()
        s4[i] = acc3[i, 1 - f] + r3[i, 1 - f].astype(f32)
        wave[c, a] = send("s4", s4.at[i], r4.at[i], (p4, p3)[a])
        acc4[i] = acc3[i, f] + r3[i, f].astype(f32)

    def double(c, a, step):
        if step > 0:
            wave[c, a].wait_recv()
        (b1, b2, b3, b4), (p1, p2, p3, p4) = roles(c)
        if step == 0:
            region, device = hp.at[c, a, b1, b2, b3, b4], (p4, p3)[a]
        elif step == 1:
            region = hp.at[c, a, b1, b2, b3] if a == 0 else hp.at[c, a, b1, b2, :, b4]
            device = (p3, p4)[a]
        elif step == 2:
            region, device = hp.at[c, a, b1, b2], (p2, p1)[a]
        else:
            region = hp.at[c, a, b1] if a == 0 else hp.at[c, a, :, b2]
            device = (p1, p2)[a]
        wave[c, a] = send(("d0", "d1", "d2", "d3")[step], region, region, device)

    def activate(c):
        wave[c, 0].wait_recv()
        wave[c, 1].wait_recv()
        b1, b2, b3, b4 = roles(c)[0]
        activated, derivative = gelu_parts(acc4[2 * c] + r4[2 * c])
        hp[c, 0, b1, b2, b3, b4] = activated.astype(bf16)
        double(c, 0, 0)
        backed = acc4[2 * c + 1] + r4[2 * c + 1]
        hp[c, 1, b1, b2, b3, b4] = (backed * derivative).astype(bf16)
        double(c, 1, 0)

    pair, cut, scattered = {}, {}, []

    def project(c, a):
        wave[c, a].wait_recv()
        low, high = rows_of(hp[c, a, :, :, :, 0]), rows_of(hp[c, a, :, :, :, 1])
        rows = jnp.concatenate([low, high], axis=1)
        value = contract(rows, (w_down, w_up_t)[a][...], 1, 0)
        part[c, a] = value.reshape(part.shape[2:])
        pair[c, a] = send("part", part.at[c, a, :, 1 - k], q0.at[c, a], sibling)

    def merge(c, a):
        pair[c, a].wait_recv()
        sy[c, a] = (part[c, a, :, k, 1 - yl] + q0[c, a, :, 1 - yl]).astype(bf16)
        cut[c, a] = send("sy", sy.at[c, a], ry.at[c, a], ypartner)
        ky[c, a] = part[c, a, :, k, yl] + q0[c, a, :, yl]

    def scatter(c):
        cut[c, 0].wait_recv()
        cut[c, 1].wait_recv()
        for s in (1, 0):
            slot = 2 * c + s
            value = ky[c, :, s] + ry[c, :, s].astype(f32)
            if slot == 0:
                own[...] = value
            else:
                ds[slot] = value.astype(bf16)
                scattered.append(send("ds", ds.at[slot], rd.at[slot], along(OFFSETS[slot])))

    stores = []

    def store(src, dst):
        stores.append(pltpu.make_async_copy(src, dst, store_sem.at[len(stores)]))
        stores[-1].start()

    def up_grad(h):
        cols = slice(h * half, (h + 1) * half)
        right = rows_of(hp[:, 1, :, :, :, h])
        up_out[:, cols] = contract(act_t[...], right, 1, 0).astype(bf16)
        store(up_out.at[:, cols], up_grad_hbm.at[:, cols])

    def down_grad(h):
        rows = slice(h * half, (h + 1) * half)
        left, right = rows_of(hp[:, 0, :, :, :, h]), rows_of(tok[1])
        down_out[rows, :] = contract(left, right, 0, 0).astype(bf16)
        store(down_out.at[rows], down_grad_hbm.at[rows])

    def begin():
        loads[0].wait()
        loads[1].wait()
        hop(0, 1)
        hop(0, -1)
        cross(0)
        hop(0, 2)
        hop(0, -2)

    def pass_on(offset):
        arrive(offset)
        if offset == 4:
            arrive(-4)
        if offset in (2, -2):
            way = -offset // 2
            hop(offset, way)
            hop(offset, 2 * way, 0 if way == 1 else 1)
        cross(slot_of(offset))

    def grads(n):
        (up_grad, down_grad)[n // 2](n % 2)

    stages = {
        "y": pass_on, "s": share, "t": flip, "ta": flip_tokens, "r1": reduce1, "r2": reduce2,
        "r3": reduce3, "r4": reduce4, "act": activate, "c1": lambda c, a: double(c, a, 1),
        "c2": lambda c, a: double(c, a, 2), "c3": lambda c, a: double(c, a, 3),
        "p": project, "m": merge, "z": scatter, "g": grads,
    }
    begin()
    loads[2].wait()
    loads[3].wait()
    for stage, *where in ORDER:
        stages[stage](*where)
    for copy in scattered:
        copy.wait_recv()
    for a, ref in ((0, out_hbm), (1, in_grad_hbm)):
        total = own[a]
        for slot in range(1, 8):
            total = total + rd[slot, a].astype(f32)
        small_out[a] = total.astype(bf16)
        store(small_out.at[a], ref)
    sent = {
        "hop": tok.at[:, 0:7, 0, 0], "cross": tok.at[:, :, 0, 0], "share": tok.at[:, :, 0],
        "s1": s1, "s2": s2, "s3": s3, "s4": s4, "d0": hp.at[:, :, 0, 0, 0, 0],
        "d1": hp.at[:, :, 0, 0, 0], "d2": hp.at[:, :, 0, 0], "d3": hp.at[:, :, 0],
        "part": q0, "sy": sy, "ds": ds.at[1:8],
    }
    for kind, ref in sent.items():
        pltpu.make_async_copy(ref, ref, send_sem.at[kinds.index(kind)]).wait()
    for copy in stores:
        copy.wait()


KINDS, COPIES = 14, 128


def place(*refs):
    arrays, results, buffers, load_sem, store_sem = refs[:4], refs[4:8], refs[8:12], refs[12], refs[13]
    loads, stores = [], []
    for src, dst, buffer in zip(arrays, results, buffers):
        rows = src.shape[0]
        step = min(rows, 256)
        for first in range(0, rows, step):
            n, part = len(loads), pl.ds(first, step)
            loads.append(pltpu.make_async_copy(src.at[part], buffer.at[part], load_sem.at[n]))
            stores.append(pltpu.make_async_copy(buffer.at[part], dst.at[part], store_sem.at[n]))
    for load in loads:
        load.start()
    for load, store in zip(loads, stores):
        load.wait()
        store.start()
    for store in stores:
        store.wait()


def shards(activations, weight_up, weight_down, out_grad):
    width, hidden = weight_up.shape
    bf16, f32 = jnp.bfloat16, jnp.float32
    assert activations.shape[0] == BLK and width == hidden

    def vmem(lead, kind):
        return pltpu.VMEM(lead + (BLK, width), kind)

    def halves(lead, kind):
        return pltpu.VMEM(lead + (BLK, hidden // 2), kind)

    pieces = 2 * CHUNKS
    scratch = [
        vmem((2, 8, 2, 2), bf16),
        pltpu.VMEM((width, 8 * CHUNKS * BLK), bf16),
        pltpu.VMEM((width, hidden), bf16), pltpu.VMEM((width, hidden), bf16),
        pltpu.VMEM((width, hidden), bf16), pltpu.VMEM((width, hidden), bf16),
        vmem((pieces, 2, 2, 2), f32), vmem((pieces, 2, 2), bf16), vmem((pieces, 2, 2), bf16),
        halves((pieces, 2, 2), f32), halves((pieces, 2, 2), bf16), halves((pieces, 2, 2), bf16),
        halves((pieces, 2), f32), halves((pieces, 2), bf16), halves((pieces, 2), bf16),
        halves((pieces,), f32), halves((pieces,), f32), halves((pieces,), f32),
        halves((CHUNKS, 2, 2, 2, 2, 2), bf16),
        vmem((CHUNKS, 2, 2, 2, 2), f32), vmem((CHUNKS, 2, 2, 2), f32),
        vmem((CHUNKS, 2, 2), f32), vmem((CHUNKS, 2, 2), bf16), vmem((CHUNKS, 2, 2), bf16),
        vmem((2,), f32), vmem((8, 2), bf16), vmem((8, 2), bf16),
        pltpu.VMEM((width, hidden), bf16), pltpu.VMEM((width, hidden), bf16), vmem((2,), bf16),
        pltpu.SemaphoreType.DMA((4,)), pltpu.SemaphoreType.DMA((6,)),
        pltpu.SemaphoreType.DMA((KINDS,)), pltpu.SemaphoreType.DMA((COPIES,)),
    ]
    small = jax.ShapeDtypeStruct(activations.shape, bf16)
    large = jax.ShapeDtypeStruct(weight_up.shape, bf16)
    results = pl.pallas_call(
        kernel,
        out_shape=(small, small, large, large),
        in_specs=[pl.BlockSpec(memory_space=pltpu.HBM)] * 4,
        out_specs=[pl.BlockSpec(memory_space=pltpu.HBM)] * 4,
        scratch_shapes=scratch,
        compiler_params=pltpu.CompilerParams(
            collective_id=0, has_side_effects=True, vmem_limit_bytes=VMEM_MIB * 1024 * 1024
        ),
        cost_estimate=pl.CostEstimate(
            flops=12 * 512 * width * hidden, bytes_accessed=8 * width * hidden, transcendentals=0
        ),
        name="layer",
    )(activations, weight_up, weight_down, out_grad)
    out, in_grad, up_grad, down_grad = results
    up_grad, down_grad, out, in_grad = pl.pallas_call(
        place,
        out_shape=(large, large, small, small),
        in_specs=[pl.BlockSpec(memory_space=pltpu.HBM)] * 4,
        out_specs=[pl.BlockSpec(memory_space=pltpu.HBM)] * 4,
        scratch_shapes=[pltpu.VMEM(result.shape, bf16) for result in (large, large, small, small)]
        + [pltpu.SemaphoreType.DMA((8,)), pltpu.SemaphoreType.DMA((8,))],
        compiler_params=pltpu.CompilerParams(vmem_limit_bytes=VMEM_MIB * 1024 * 1024),
        name="place",
    )(up_grad, down_grad, out, in_grad)
    return out, in_grad, up_grad, down_grad


VMEM_MIB = 60


def solution(mesh):
    placed = (
        P(("depth", "col"), "row"),
        P("row", ("depth", "col")),
        P(("depth", "col"), "row"),
        P(("depth", "col"), "row"),
    )
    return jax.shard_map(
        shards,
        mesh=mesh,
        in_specs=placed,
        out_specs=(
            P(("depth", "col"), "row"),
            P(("depth", "col"), "row"),
            P("row", ("depth", "col")),
            P(("depth", "col"), "row"),
        ),
        check_vma=False,
    )
```

```python
import jax
import jax.numpy as jnp
from jax import lax
from jax.experimental import pallas as pl
from jax.experimental.pallas import tpu as pltpu
from jax.sharding import PartitionSpec as P

tanh_scale = 0.7978845608028654
cubic_coeff = 0.044715

OFFSETS = (0, 1, -1, 2, -2, 3, -3, 4)
CHUNKS = 4
BLK = 16


ORDER = (
    ("y", 1), ("s", 0), ("y", -1), ("s", 1), ("y", 2), ("y", -2), ("s", 2),
    ("r1", 0), ("s", 3), ("y", 3), ("r1", 1), ("y", 4), ("y", -3), ("s", 4),
    ("s", 5), ("r2", 0), ("r1", 2), ("s", 6), ("s", 7), ("r2", 1), ("r3", 0),
    ("r1", 3), ("r2", 2), ("r3", 1), ("r4", 0), ("r2", 3), ("r3", 2), ("r4", 1),
    ("r3", 3), ("r4", 2), ("ta", 0), ("act", 1), ("r4", 3), ("act", 2), ("ta", 1),
    ("c1", 1), ("act", 0), ("c1", 2), ("c2", 1), ("ta", 2), ("act", 3), ("c2", 2),
    ("c3", 1), ("ta", 3), ("c1", 3), ("c3", 2), ("c1", 0), ("c2", 3), ("p", 1),
    ("c2", 0), ("p", 2), ("c3", 3), ("m", 1), ("c3", 0), ("m", 2), ("p", 3),
    ("z", 1), ("p", 0), ("z", 2), ("m", 3), ("m", 0), ("z", 3), ("z", 0),
    ("g", 0), ("g", 1), ("g", 2), ("g", 3),
)


def slot_of(offset):
    return OFFSETS.index(4 if offset == -4 else offset)


def gelu_parts(preact):
    inner = tanh_scale * (preact + cubic_coeff * preact * preact * preact)
    hyper = jnp.tanh(inner)
    activated = 0.5 * preact * (1.0 + hyper)
    derivative = 0.5 * (1.0 + hyper) + 0.5 * preact * (1.0 - hyper * hyper) * tanh_scale * (
        1.0 + 3.0 * cubic_coeff * preact * preact
    )
    return (activated, derivative)


def contract(left, right, left_dim, right_dim):
    return lax.dot_general(
        left, right, (((left_dim,), (right_dim,)), ((), ())), preferred_element_type=jnp.float32
    )


def rows_of(value):
    return value.reshape((-1, value.shape[-1]))


def kernel(
    act_hbm, up_hbm, down_hbm, cot_hbm,
    out_hbm, in_grad_hbm, up_grad_hbm, down_grad_hbm,
    tok, act_t, w_up, w_down, acc0, s1, r1, acc2, s2, r2, acc3, s3, r3, acc4, s4, r4,
    hp, part, q0, ky, sy, ry, own, ds, rd, up_out, down_out, small_out,
    load_sem, store_sem, send_sem, recv_sem,
):
    bf16, f32 = jnp.bfloat16, jnp.float32
    width = tok.shape[-1]
    half = width // 2
    depth, row, z = lax.axis_index("depth"), lax.axis_index("row"), lax.axis_index("col")
    yl, k = depth // 2, depth % 2
    x, yh = row // 4, row % 4
    f1x, f2x = (x + x // 2) % 2, x // 2
    f1y, f2y = (yh + yh // 2) % 2, yh // 2
    p1x, p2x = {"row": (x + 1 - 2 * (x % 2)) * 4 + yh}, {"row": (3 - x) * 4 + yh}
    p1y, p2y = {"row": x * 4 + yh + 1 - 2 * (yh % 2)}, {"row": x * 4 + 3 - yh}
    sibling, ypartner = {"depth": yl * 2 + 1 - k}, {"depth": (1 - yl) * 2 + k}

    def along(offset):
        return {"col": (z + offset + 8) % 8}

    partners = [sibling, ypartner, p1x, p2x, p1y, p2y] + [along(o) for o in OFFSETS[1:]]

    started, kinds = [], []

    def send(kind, src, dst, device):
        n = len(started)
        if kind not in kinds:
            kinds.append(kind)
        copy = pltpu.make_async_remote_copy(
            src_ref=src, dst_ref=dst, send_sem=send_sem.at[kinds.index(kind)],
            recv_sem=recv_sem.at[n],
            device_id=device, device_id_type=pl.DeviceIdType.MESH,
        )
        copy.start()
        started.append(copy)
        return copy

    loads = [
        pltpu.make_async_copy(act_hbm, tok.at[0, 0, k, yl], load_sem.at[0]),
        pltpu.make_async_copy(cot_hbm, tok.at[1, 0, k, yl], load_sem.at[1]),
        pltpu.make_async_copy(up_hbm, w_up, load_sem.at[2]),
        pltpu.make_async_copy(down_hbm, w_down, load_sem.at[3]),
    ]
    for load in loads:
        load.start()
    barrier = pltpu.get_barrier_semaphore()
    for device in partners:
        pl.semaphore_signal(barrier, inc=1, device_id=device, device_id_type=pl.DeviceIdType.MESH)
    pl.semaphore_wait(barrier, len(partners))

    flow, across, shared = {}, {}, {}

    def block(slot, a=slice(None)):
        return tok.at[a, slot, k, yl]

    def hop(offset, way, a=slice(None)):
        target = offset - way
        flow[target] = flow.get(target, []) + [
            send("hop", block(slot_of(offset), a), block(slot_of(target), a), along(way))
        ]

    def cross(slot):
        across[slot] = send("cross", block(slot), block(slot), ypartner)

    def arrive(offset):
        for copy in flow[offset]:
            copy.wait_recv()

    def share(slot):
        across[slot].wait_recv()
        mine = tok.at[:, slot, k]
        shared[slot] = send("share", mine, mine, sibling)

    wave = {}

    def flip_tokens(c):
        act_t[:, c * 8 * BLK : (c + 1) * 8 * BLK] = rows_of(tok[0, 2 * c : 2 * c + 2]).T

    def reduce1(c):
        for slot in (2 * c, 2 * c + 1):
            shared[slot].wait_recv()
        for a in range(2):
            i, f = 2 * c + a, (f1x, f2x)[a]
            rows = rows_of(tok[a, 2 * c : 2 * c + 2])
            value = contract(rows, w_up[...], 1, 0) if a == 0 else contract(rows, w_down[...], 1, 1)
            acc0[i] = value.reshape(acc0.shape[1:])
            s1[i] = (acc0[i, 1 - f] if a == 0 else acc0[i, :, 1 - f]).astype(bf16)
            wave[c, a] = send("s1", s1.at[i], r1.at[i], (p1x, p2x)[a])

    def reduce2(c):
        for a in range(2):
            i, f, g = 2 * c + a, (f1x, f2x)[a], (f2x, f1x)[a]
            wave[c, a].wait_recv()

            def total(n):
                kept = acc0[i, f, n] if a == 0 else acc0[i, n, f]
                return kept + r1[i, n].astype(f32)

            value = total(1 - g).astype(bf16)
            s2[i, :, 0] = value[..., :half]
            s2[i, :, 1] = value[..., half:]
            wave[c, a] = send("s2", s2.at[i], r2.at[i], (p2x, p1x)[a])
            value = total(g)
            acc2[i, :, 0] = value[..., :half]
            acc2[i, :, 1] = value[..., half:]

    def reduce3(c):
        for a in range(2):
            i, f = 2 * c + a, (f1y, f2y)[a]
            wave[c, a].wait_recv()

            def total(n):
                if a == 0:
                    return acc2[i, n] + r2[i, n].astype(f32)
                return acc2[i, :, n] + r2[i, :, n].astype(f32)

            s3[i] = total(1 - f).astype(bf16)
            wave[c, a] = send("s3", s3.at[i], r3.at[i], (p1y, p2y)[a])
            acc3[i] = total(f)

    def reduce4(c):
        for a in range(2):
            i, f = 2 * c + a, (f2y, f1y)[a]
            wave[c, a].wait_recv()
            s4[i] = acc3[i, 1 - f] + r3[i, 1 - f].astype(f32)
            wave[c, a] = send("s4", s4.at[i], r4.at[i], (p2y, p1y)[a])
            acc4[i] = acc3[i, f] + r3[i, f].astype(f32)

    def double(c, step):
        for a in range(2):
            if step > 0:
                wave[c, a].wait_recv()
            if step == 0:
                region, device = hp.at[c, a, f1x, f2x, f1y, f2y], (p2y, p1y)[a]
            elif step == 1:
                region = hp.at[c, a, f1x, f2x, f1y] if a == 0 else hp.at[c, a, f1x, f2x, :, f2y]
                device = (p1y, p2y)[a]
            elif step == 2:
                region, device = hp.at[c, a, f1x, f2x], (p2x, p1x)[a]
            else:
                region = hp.at[c, a, f1x] if a == 0 else hp.at[c, a, :, f2x]
                device = (p1x, p2x)[a]
            wave[c, a] = send(("d0", "d1", "d2", "d3")[step], region, region, device)

    def activate(c):
        wave[c, 0].wait_recv()
        wave[c, 1].wait_recv()
        activated, derivative = gelu_parts(acc4[2 * c] + r4[2 * c])
        hp[c, 0, f1x, f2x, f1y, f2y] = activated.astype(bf16)
        backed = acc4[2 * c + 1] + r4[2 * c + 1]
        hp[c, 1, f1x, f2x, f1y, f2y] = (backed * derivative).astype(bf16)
        double(c, 0)

    pair, cut, scattered = {}, {}, []

    def project(c):
        for a in range(2):
            wave[c, a].wait_recv()
            low, high = rows_of(hp[c, a, :, :, :, 0]), rows_of(hp[c, a, :, :, :, 1])
            rows = jnp.concatenate([low, high], axis=1)
            value = contract(rows, w_down[...], 1, 0) if a == 0 else contract(rows, w_up[...], 1, 1)
            part[c, a] = value.reshape(part.shape[2:])
            pair[c, a] = send("part", part.at[c, a, :, 1 - k], q0.at[c, a], sibling)

    def merge(c):
        for a in range(2):
            pair[c, a].wait_recv()
            sy[c, a] = (part[c, a, :, k, 1 - yl] + q0[c, a, :, 1 - yl]).astype(bf16)
        cut[c] = send("sy", sy.at[c], ry.at[c], ypartner)
        for a in range(2):
            ky[c, a] = part[c, a, :, k, yl] + q0[c, a, :, yl]

    def scatter(c):
        cut[c].wait_recv()
        for s in (1, 0):
            slot = 2 * c + s
            value = ky[c, :, s] + ry[c, :, s].astype(f32)
            if slot == 0:
                own[...] = value
            else:
                ds[slot] = value.astype(bf16)
                scattered.append(send("ds", ds.at[slot], rd.at[slot], along(OFFSETS[slot])))

    stores = []

    def store(src, dst):
        stores.append(pltpu.make_async_copy(src, dst, store_sem.at[len(stores)]))
        stores[-1].start()

    def up_grad(h):
        cols = slice(h * half, (h + 1) * half)
        right = rows_of(hp[:, 1, :, :, :, h])
        up_out[:, cols] = contract(act_t[...], right, 1, 0).astype(bf16)
        store(up_out.at[:, cols], up_grad_hbm.at[:, cols])

    def down_grad(h):
        rows = slice(h * half, (h + 1) * half)
        left, right = rows_of(hp[:, 0, :, :, :, h]), rows_of(tok[1])
        down_out[rows, :] = contract(left, right, 0, 0).astype(bf16)
        store(down_out.at[rows], down_grad_hbm.at[rows])

    def begin():
        loads[0].wait()
        loads[1].wait()
        hop(0, 1)
        hop(0, -1)
        cross(0)
        hop(0, 2)
        hop(0, -2)

    def pass_on(offset):
        arrive(offset)
        if offset == 4:
            arrive(-4)
        if offset in (2, -2):
            way = -offset // 2
            hop(offset, way)
            hop(offset, 2 * way, 0 if way == 1 else 1)
        cross(slot_of(offset))

    def grads(n):
        (up_grad, down_grad)[n // 2](n % 2)

    stages = {
        "y": pass_on, "s": share, "ta": flip_tokens, "r1": reduce1, "r2": reduce2, "r3": reduce3, "r4": reduce4,
        "act": activate, "c1": lambda c: double(c, 1), "c2": lambda c: double(c, 2),
        "c3": lambda c: double(c, 3), "p": project, "m": merge, "z": scatter, "g": grads,
    }
    begin()
    loads[2].wait()
    loads[3].wait()
    for stage, index in ORDER:
        stages[stage](index)
    for copy in scattered:
        copy.wait_recv()
    for a, ref in ((0, out_hbm), (1, in_grad_hbm)):
        total = own[a]
        for slot in range(1, 8):
            total = total + rd[slot, a].astype(f32)
        small_out[a] = total.astype(bf16)
        store(small_out.at[a], ref)
    sent = {
        "hop": tok.at[:, 0:7, 0, 0], "cross": tok.at[:, :, 0, 0], "share": tok.at[:, :, 0],
        "s1": s1, "s2": s2, "s3": s3, "s4": s4, "d0": hp.at[:, :, 0, 0, 0, 0],
        "d1": hp.at[:, :, 0, 0, 0], "d2": hp.at[:, :, 0, 0], "d3": hp.at[:, :, 0],
        "part": q0, "sy": sy, "ds": ds.at[1:8],
    }
    for kind, ref in sent.items():
        pltpu.make_async_copy(ref, ref, send_sem.at[kinds.index(kind)]).wait()
    for copy in stores:
        copy.wait()


KINDS, COPIES = 14, 128


def place(*refs):
    arrays, results, buffers, load_sem, store_sem = refs[:4], refs[4:8], refs[8:12], refs[12], refs[13]
    loads, stores = [], []
    for src, dst, buffer in zip(arrays, results, buffers):
        rows = src.shape[0]
        step = min(rows, 256)
        for first in range(0, rows, step):
            n, part = len(loads), pl.ds(first, step)
            loads.append(pltpu.make_async_copy(src.at[part], buffer.at[part], load_sem.at[n]))
            stores.append(pltpu.make_async_copy(buffer.at[part], dst.at[part], store_sem.at[n]))
    for load in loads:
        load.start()
    for load, store in zip(loads, stores):
        load.wait()
        store.start()
    for store in stores:
        store.wait()


def shards(activations, weight_up, weight_down, out_grad):
    width, hidden = weight_up.shape
    bf16, f32 = jnp.bfloat16, jnp.float32
    assert activations.shape[0] == BLK and width == hidden

    def vmem(lead, kind):
        return pltpu.VMEM(lead + (BLK, width), kind)

    def halves(lead, kind):
        return pltpu.VMEM(lead + (BLK, hidden // 2), kind)

    pieces = 2 * CHUNKS
    scratch = [
        vmem((2, 8, 2, 2), bf16),
        pltpu.VMEM((width, 8 * CHUNKS * BLK), bf16),
        pltpu.VMEM((width, hidden), bf16), pltpu.VMEM((width, hidden), bf16),
        vmem((pieces, 2, 2, 2), f32), vmem((pieces, 2, 2), bf16), vmem((pieces, 2, 2), bf16),
        halves((pieces, 2, 2), f32), halves((pieces, 2, 2), bf16), halves((pieces, 2, 2), bf16),
        halves((pieces, 2), f32), halves((pieces, 2), bf16), halves((pieces, 2), bf16),
        halves((pieces,), f32), halves((pieces,), f32), halves((pieces,), f32),
        halves((CHUNKS, 2, 2, 2, 2, 2), bf16),
        vmem((CHUNKS, 2, 2, 2, 2), f32), vmem((CHUNKS, 2, 2, 2), f32),
        vmem((CHUNKS, 2, 2), f32), vmem((CHUNKS, 2, 2), bf16), vmem((CHUNKS, 2, 2), bf16),
        vmem((2,), f32), vmem((8, 2), bf16), vmem((8, 2), bf16),
        pltpu.VMEM((width, hidden), bf16), pltpu.VMEM((width, hidden), bf16), vmem((2,), bf16),
        pltpu.SemaphoreType.DMA((4,)), pltpu.SemaphoreType.DMA((6,)),
        pltpu.SemaphoreType.DMA((KINDS,)), pltpu.SemaphoreType.DMA((COPIES,)),
    ]
    small = jax.ShapeDtypeStruct(activations.shape, bf16)
    large = jax.ShapeDtypeStruct(weight_up.shape, bf16)
    results = pl.pallas_call(
        kernel,
        out_shape=(small, small, large, large),
        in_specs=[pl.BlockSpec(memory_space=pltpu.HBM)] * 4,
        out_specs=[pl.BlockSpec(memory_space=pltpu.HBM)] * 4,
        scratch_shapes=scratch,
        compiler_params=pltpu.CompilerParams(
            collective_id=0, has_side_effects=True, vmem_limit_bytes=VMEM_MIB * 1024 * 1024
        ),
        cost_estimate=pl.CostEstimate(
            flops=12 * 512 * width * hidden, bytes_accessed=8 * width * hidden, transcendentals=0
        ),
        name="layer",
    )(activations, weight_up, weight_down, out_grad)
    out, in_grad, up_grad, down_grad = results
    up_grad, down_grad, out, in_grad = pl.pallas_call(
        place,
        out_shape=(large, large, small, small),
        in_specs=[pl.BlockSpec(memory_space=pltpu.HBM)] * 4,
        out_specs=[pl.BlockSpec(memory_space=pltpu.HBM)] * 4,
        scratch_shapes=[pltpu.VMEM(result.shape, bf16) for result in (large, large, small, small)]
        + [pltpu.SemaphoreType.DMA((8,)), pltpu.SemaphoreType.DMA((8,))],
        compiler_params=pltpu.CompilerParams(vmem_limit_bytes=VMEM_MIB * 1024 * 1024),
        name="place",
    )(up_grad, down_grad, out, in_grad)
    return out, in_grad, up_grad, down_grad


VMEM_MIB = 60


def solution(mesh):
    placed = (
        P(("depth", "col"), "row"),
        P("row", ("depth", "col")),
        P(("depth", "col"), "row"),
        P(("depth", "col"), "row"),
    )
    return jax.shard_map(
        shards,
        mesh=mesh,
        in_specs=placed,
        out_specs=(
            P(("depth", "col"), "row"),
            P(("depth", "col"), "row"),
            P("row", ("depth", "col")),
            P(("depth", "col"), "row"),
        ),
        check_vma=False,
    )
```

```python
import jax
import jax.numpy as jnp
from jax import lax
from jax.experimental import pallas as pl
from jax.experimental.pallas import tpu as pltpu
from jax.sharding import PartitionSpec as P

tanh_scale = 0.7978845608028654
cubic_coeff = 0.044715

OFFSETS = (0, 1, -1, 2, -2, 3, -3, 4)
CHUNKS = 4
BLK = 16


ORDER = (
    ("y", 1), ("y", -1), ("s", 0), ("s", 1), ("s", 2), ("y", 2), ("y", -2),
    ("r1", 0), ("s", 3), ("s", 4), ("y", 3), ("y", -3), ("r1", 1), ("s", 5),
    ("s", 6), ("y", 4), ("s", 7), ("r2", 0), ("r1", 2), ("r2", 1), ("r3", 0),
    ("r1", 3), ("r2", 2), ("r3", 1), ("r4", 0), ("r2", 3), ("r3", 2), ("r4", 1),
    ("r3", 3), ("r4", 2), ("ta", 0), ("act", 1), ("r4", 3), ("act", 2), ("ta", 1),
    ("c1", 1), ("act", 0), ("c1", 2), ("c2", 1), ("ta", 2), ("act", 3), ("c2", 2),
    ("c3", 1), ("ta", 3), ("c1", 3), ("c3", 2), ("c1", 0), ("c2", 3), ("p", 1),
    ("c2", 0), ("p", 2), ("c3", 3), ("m", 1), ("c3", 0), ("m", 2), ("p", 3),
    ("z", 1), ("p", 0), ("z", 2), ("m", 3), ("m", 0), ("z", 3), ("z", 0),
    ("g", 0), ("g", 1), ("g", 2), ("g", 3),
)


def slot_of(offset):
    return OFFSETS.index(4 if offset == -4 else offset)


def gelu_parts(preact):
    inner = tanh_scale * (preact + cubic_coeff * preact * preact * preact)
    hyper = jnp.tanh(inner)
    activated = 0.5 * preact * (1.0 + hyper)
    derivative = 0.5 * (1.0 + hyper) + 0.5 * preact * (1.0 - hyper * hyper) * tanh_scale * (
        1.0 + 3.0 * cubic_coeff * preact * preact
    )
    return (activated, derivative)


def contract(left, right, left_dim, right_dim):
    return lax.dot_general(
        left, right, (((left_dim,), (right_dim,)), ((), ())), preferred_element_type=jnp.float32
    )


def rows_of(value):
    return value.reshape((-1, value.shape[-1]))


def kernel(
    act_hbm, up_hbm, down_hbm, cot_hbm,
    out_hbm, in_grad_hbm, up_grad_hbm, down_grad_hbm,
    tok, act_t, w_up, w_down, acc0, s1, r1, acc2, s2, r2, acc3, s3, r3, acc4, s4, r4,
    hp, part, q0, ky, sy, ry, own, ds, rd, up_out, down_out, small_out,
    load_sem, store_sem, send_sem, recv_sem,
):
    bf16, f32 = jnp.bfloat16, jnp.float32
    width = tok.shape[-1]
    half = width // 2
    depth, row, z = lax.axis_index("depth"), lax.axis_index("row"), lax.axis_index("col")
    yl, k = depth // 2, depth % 2
    x, yh = row // 4, row % 4
    f1x, f2x = (x + x // 2) % 2, x // 2
    f1y, f2y = (yh + yh // 2) % 2, yh // 2
    p1x, p2x = {"row": (x + 1 - 2 * (x % 2)) * 4 + yh}, {"row": (3 - x) * 4 + yh}
    p1y, p2y = {"row": x * 4 + yh + 1 - 2 * (yh % 2)}, {"row": x * 4 + 3 - yh}
    sibling, ypartner = {"depth": yl * 2 + 1 - k}, {"depth": (1 - yl) * 2 + k}

    def along(offset):
        return {"col": (z + offset + 8) % 8}

    partners = [sibling, ypartner, p1x, p2x, p1y, p2y] + [along(o) for o in OFFSETS[1:]]

    started, kinds = [], []

    def send(kind, src, dst, device):
        n = len(started)
        if kind not in kinds:
            kinds.append(kind)
        copy = pltpu.make_async_remote_copy(
            src_ref=src, dst_ref=dst, send_sem=send_sem.at[kinds.index(kind)],
            recv_sem=recv_sem.at[n],
            device_id=device, device_id_type=pl.DeviceIdType.MESH,
        )
        copy.start()
        started.append(copy)
        return copy

    loads = [
        pltpu.make_async_copy(act_hbm, tok.at[0, 0, k, yl], load_sem.at[0]),
        pltpu.make_async_copy(cot_hbm, tok.at[1, 0, k, yl], load_sem.at[1]),
        pltpu.make_async_copy(up_hbm, w_up, load_sem.at[2]),
        pltpu.make_async_copy(down_hbm, w_down, load_sem.at[3]),
    ]
    for load in loads:
        load.start()
    barrier = pltpu.get_barrier_semaphore()
    for device in partners:
        pl.semaphore_signal(barrier, inc=1, device_id=device, device_id_type=pl.DeviceIdType.MESH)
    pl.semaphore_wait(barrier, len(partners))

    flow, shared = {}, {}

    def slab(slot, a=slice(None)):
        return tok.at[a, slot, k]

    def hop(offset, way, a=slice(None)):
        target = offset - way
        flow[target] = send("hop", slab(slot_of(offset), a), slab(slot_of(target), a), along(way))

    def share(slot):
        shared[slot] = send("share", slab(slot), slab(slot), sibling)

    wave = {}

    def flip_tokens(c):
        act_t[:, c * 8 * BLK : (c + 1) * 8 * BLK] = rows_of(tok[0, 2 * c : 2 * c + 2]).T

    def reduce1(c):
        for slot in (2 * c, 2 * c + 1):
            shared[slot].wait_recv()
        for a in range(2):
            i, f = 2 * c + a, (f1x, f2x)[a]
            rows = rows_of(tok[a, 2 * c : 2 * c + 2])
            value = contract(rows, w_up[...], 1, 0) if a == 0 else contract(rows, w_down[...], 1, 1)
            acc0[i] = value.reshape(acc0.shape[1:])
            s1[i] = (acc0[i, 1 - f] if a == 0 else acc0[i, :, 1 - f]).astype(bf16)
            wave[c, a] = send("s1", s1.at[i], r1.at[i], (p1x, p2x)[a])

    def reduce2(c):
        for a in range(2):
            i, f, g = 2 * c + a, (f1x, f2x)[a], (f2x, f1x)[a]
            wave[c, a].wait_recv()

            def total(n):
                kept = acc0[i, f, n] if a == 0 else acc0[i, n, f]
                return kept + r1[i, n].astype(f32)

            value = total(1 - g).astype(bf16)
            s2[i, :, 0] = value[..., :half]
            s2[i, :, 1] = value[..., half:]
            wave[c, a] = send("s2", s2.at[i], r2.at[i], (p2x, p1x)[a])
            value = total(g)
            acc2[i, :, 0] = value[..., :half]
            acc2[i, :, 1] = value[..., half:]

    def reduce3(c):
        for a in range(2):
            i, f = 2 * c + a, (f1y, f2y)[a]
            wave[c, a].wait_recv()

            def total(n):
                if a == 0:
                    return acc2[i, n] + r2[i, n].astype(f32)
                return acc2[i, :, n] + r2[i, :, n].astype(f32)

            s3[i] = total(1 - f).astype(bf16)
            wave[c, a] = send("s3", s3.at[i], r3.at[i], (p1y, p2y)[a])
            acc3[i] = total(f)

    def reduce4(c):
        for a in range(2):
            i, f = 2 * c + a, (f2y, f1y)[a]
            wave[c, a].wait_recv()
            s4[i] = acc3[i, 1 - f] + r3[i, 1 - f].astype(f32)
            wave[c, a] = send("s4", s4.at[i], r4.at[i], (p2y, p1y)[a])
            acc4[i] = acc3[i, f] + r3[i, f].astype(f32)

    def double(c, step):
        for a in range(2):
            if step > 0:
                wave[c, a].wait_recv()
            if step == 0:
                region, device = hp.at[c, a, f1x, f2x, f1y, f2y], (p2y, p1y)[a]
            elif step == 1:
                region = hp.at[c, a, f1x, f2x, f1y] if a == 0 else hp.at[c, a, f1x, f2x, :, f2y]
                device = (p1y, p2y)[a]
            elif step == 2:
                region, device = hp.at[c, a, f1x, f2x], (p2x, p1x)[a]
            else:
                region = hp.at[c, a, f1x] if a == 0 else hp.at[c, a, :, f2x]
                device = (p1x, p2x)[a]
            wave[c, a] = send(("d0", "d1", "d2", "d3")[step], region, region, device)

    def activate(c):
        wave[c, 0].wait_recv()
        wave[c, 1].wait_recv()
        activated, derivative = gelu_parts(acc4[2 * c] + r4[2 * c])
        hp[c, 0, f1x, f2x, f1y, f2y] = activated.astype(bf16)
        backed = acc4[2 * c + 1] + r4[2 * c + 1]
        hp[c, 1, f1x, f2x, f1y, f2y] = (backed * derivative).astype(bf16)
        double(c, 0)

    pair, cut, scattered = {}, {}, []

    def project(c):
        for a in range(2):
            wave[c, a].wait_recv()
            low, high = rows_of(hp[c, a, :, :, :, 0]), rows_of(hp[c, a, :, :, :, 1])
            rows = jnp.concatenate([low, high], axis=1)
            value = contract(rows, w_down[...], 1, 0) if a == 0 else contract(rows, w_up[...], 1, 1)
            part[c, a] = value.reshape(part.shape[2:])
            pair[c, a] = send("part", part.at[c, a, :, 1 - k], q0.at[c, a], sibling)

    def merge(c):
        for a in range(2):
            pair[c, a].wait_recv()
            sy[c, a] = (part[c, a, :, k, 1 - yl] + q0[c, a, :, 1 - yl]).astype(bf16)
        cut[c] = send("sy", sy.at[c], ry.at[c], ypartner)
        for a in range(2):
            ky[c, a] = part[c, a, :, k, yl] + q0[c, a, :, yl]

    def scatter(c):
        cut[c].wait_recv()
        for s in (1, 0):
            slot = 2 * c + s
            value = ky[c, :, s] + ry[c, :, s].astype(f32)
            if slot == 0:
                own[...] = value
            else:
                ds[slot] = value.astype(bf16)
                scattered.append(send("ds", ds.at[slot], rd.at[slot], along(OFFSETS[slot])))

    stores = []

    def store(src, dst):
        stores.append(pltpu.make_async_copy(src, dst, store_sem.at[len(stores)]))
        stores[-1].start()

    def up_grad(h):
        cols = slice(h * half, (h + 1) * half)
        right = rows_of(hp[:, 1, :, :, :, h])
        up_out[:, cols] = contract(act_t[...], right, 1, 0).astype(bf16)
        store(up_out.at[:, cols], up_grad_hbm.at[:, cols])

    def down_grad(h):
        rows = slice(h * half, (h + 1) * half)
        left, right = rows_of(hp[:, 0, :, :, :, h]), rows_of(tok[1])
        down_out[rows, :] = contract(left, right, 0, 0).astype(bf16)
        store(down_out.at[rows], down_grad_hbm.at[rows])

    def begin():
        loads[0].wait()
        loads[1].wait()
        mine = tok.at[:, 0, k, yl]
        send("cross", mine, mine, ypartner).wait_recv()
        hop(0, 1)
        hop(0, -1)

    def pass_on(offset):
        flow[offset].wait_recv()
        if offset == 4:
            flow[-4].wait_recv()
        else:
            way = -1 if offset > 0 else 1
            hop(offset, way, slice(None) if abs(offset) < 3 else (0 if way == 1 else 1))

    def grads(n):
        (up_grad, down_grad)[n // 2](n % 2)

    stages = {
        "y": pass_on, "s": share, "ta": flip_tokens, "r1": reduce1, "r2": reduce2, "r3": reduce3, "r4": reduce4,
        "act": activate, "c1": lambda c: double(c, 1), "c2": lambda c: double(c, 2),
        "c3": lambda c: double(c, 3), "p": project, "m": merge, "z": scatter, "g": grads,
    }
    begin()
    loads[2].wait()
    loads[3].wait()
    for stage, index in ORDER:
        stages[stage](index)
    for copy in scattered:
        copy.wait_recv()
    for a, ref in ((0, out_hbm), (1, in_grad_hbm)):
        total = own[a]
        for slot in range(1, 8):
            total = total + rd[slot, a].astype(f32)
        small_out[a] = total.astype(bf16)
        store(small_out.at[a], ref)
    sent = {
        "hop": tok.at[:, 0:7, 0], "cross": tok.at[:, 0, 0, 0], "share": tok.at[:, :, 0],
        "s1": s1, "s2": s2, "s3": s3, "s4": s4, "d0": hp.at[:, :, 0, 0, 0, 0],
        "d1": hp.at[:, :, 0, 0, 0], "d2": hp.at[:, :, 0, 0], "d3": hp.at[:, :, 0],
        "part": q0, "sy": sy, "ds": ds.at[1:8],
    }
    for kind, ref in sent.items():
        pltpu.make_async_copy(ref, ref, send_sem.at[kinds.index(kind)]).wait()
    for copy in stores:
        copy.wait()


KINDS, COPIES = 14, 128


def place(*refs):
    arrays, results, buffers, load_sem, store_sem = refs[:4], refs[4:8], refs[8:12], refs[12], refs[13]
    loads, stores = [], []
    for src, dst, buffer in zip(arrays, results, buffers):
        rows = src.shape[0]
        step = min(rows, 256)
        for first in range(0, rows, step):
            n, part = len(loads), pl.ds(first, step)
            loads.append(pltpu.make_async_copy(src.at[part], buffer.at[part], load_sem.at[n]))
            stores.append(pltpu.make_async_copy(buffer.at[part], dst.at[part], store_sem.at[n]))
    for load in loads:
        load.start()
    for load, store in zip(loads, stores):
        load.wait()
        store.start()
    for store in stores:
        store.wait()


def shards(activations, weight_up, weight_down, out_grad):
    width, hidden = weight_up.shape
    bf16, f32 = jnp.bfloat16, jnp.float32
    assert activations.shape[0] == BLK and width == hidden

    def vmem(lead, kind):
        return pltpu.VMEM(lead + (BLK, width), kind)

    def halves(lead, kind):
        return pltpu.VMEM(lead + (BLK, hidden // 2), kind)

    pieces = 2 * CHUNKS
    scratch = [
        vmem((2, 8, 2, 2), bf16),
        pltpu.VMEM((width, 8 * CHUNKS * BLK), bf16),
        pltpu.VMEM((width, hidden), bf16), pltpu.VMEM((width, hidden), bf16),
        vmem((pieces, 2, 2, 2), f32), vmem((pieces, 2, 2), bf16), vmem((pieces, 2, 2), bf16),
        halves((pieces, 2, 2), f32), halves((pieces, 2, 2), bf16), halves((pieces, 2, 2), bf16),
        halves((pieces, 2), f32), halves((pieces, 2), bf16), halves((pieces, 2), bf16),
        halves((pieces,), f32), halves((pieces,), f32), halves((pieces,), f32),
        halves((CHUNKS, 2, 2, 2, 2, 2), bf16),
        vmem((CHUNKS, 2, 2, 2, 2), f32), vmem((CHUNKS, 2, 2, 2), f32),
        vmem((CHUNKS, 2, 2), f32), vmem((CHUNKS, 2, 2), bf16), vmem((CHUNKS, 2, 2), bf16),
        vmem((2,), f32), vmem((8, 2), bf16), vmem((8, 2), bf16),
        pltpu.VMEM((width, hidden), bf16), pltpu.VMEM((width, hidden), bf16), vmem((2,), bf16),
        pltpu.SemaphoreType.DMA((4,)), pltpu.SemaphoreType.DMA((6,)),
        pltpu.SemaphoreType.DMA((KINDS,)), pltpu.SemaphoreType.DMA((COPIES,)),
    ]
    small = jax.ShapeDtypeStruct(activations.shape, bf16)
    large = jax.ShapeDtypeStruct(weight_up.shape, bf16)
    results = pl.pallas_call(
        kernel,
        out_shape=(small, small, large, large),
        in_specs=[pl.BlockSpec(memory_space=pltpu.HBM)] * 4,
        out_specs=[pl.BlockSpec(memory_space=pltpu.HBM)] * 4,
        scratch_shapes=scratch,
        compiler_params=pltpu.CompilerParams(
            collective_id=0, has_side_effects=True, vmem_limit_bytes=VMEM_MIB * 1024 * 1024
        ),
        cost_estimate=pl.CostEstimate(
            flops=12 * 512 * width * hidden, bytes_accessed=8 * width * hidden, transcendentals=0
        ),
        name="layer",
    )(activations, weight_up, weight_down, out_grad)
    out, in_grad, up_grad, down_grad = results
    up_grad, down_grad, out, in_grad = pl.pallas_call(
        place,
        out_shape=(large, large, small, small),
        in_specs=[pl.BlockSpec(memory_space=pltpu.HBM)] * 4,
        out_specs=[pl.BlockSpec(memory_space=pltpu.HBM)] * 4,
        scratch_shapes=[pltpu.VMEM(result.shape, bf16) for result in (large, large, small, small)]
        + [pltpu.SemaphoreType.DMA((8,)), pltpu.SemaphoreType.DMA((8,))],
        compiler_params=pltpu.CompilerParams(vmem_limit_bytes=VMEM_MIB * 1024 * 1024),
        name="place",
    )(up_grad, down_grad, out, in_grad)
    return out, in_grad, up_grad, down_grad


VMEM_MIB = 60


def solution(mesh):
    placed = (
        P(("depth", "col"), "row"),
        P("row", ("depth", "col")),
        P(("depth", "col"), "row"),
        P(("depth", "col"), "row"),
    )
    return jax.shard_map(
        shards,
        mesh=mesh,
        in_specs=placed,
        out_specs=(
            P(("depth", "col"), "row"),
            P(("depth", "col"), "row"),
            P("row", ("depth", "col")),
            P(("depth", "col"), "row"),
        ),
        check_vma=False,
    )
```

```python
import jax
import jax.numpy as jnp
from jax import lax
from jax.experimental import pallas as pl
from jax.experimental.pallas import tpu as pltpu
from jax.sharding import PartitionSpec as P

tanh_scale = 0.7978845608028654
cubic_coeff = 0.044715

OFFSETS = (0, 1, -1, 2, -2, 3, -3, 4)
CHUNKS = 4
BLK = 16


ORDER = (
    ("y", 1), ("y", -1), ("s", 0), ("y", 2), ("y", -2), ("r1", 0), ("s", 1),
    ("y", 3), ("r1", 1), ("y", 4), ("y", -3), ("s", 2), ("r2", 0), ("r1", 2),
    ("s", 3), ("r2", 1), ("r3", 0), ("r1", 3), ("r2", 2), ("r3", 1), ("r4", 0),
    ("r2", 3), ("r3", 2), ("r4", 1), ("r3", 3), ("r4", 2), ("ta", 0), ("act", 1),
    ("r4", 3), ("act", 2), ("ta", 1), ("c1", 1), ("act", 0), ("c1", 2), ("c2", 1),
    ("ta", 2), ("act", 3), ("c2", 2), ("c3", 1), ("ta", 3), ("c1", 3), ("c3", 2),
    ("c1", 0), ("c2", 3), ("p", 1), ("c2", 0), ("p", 2), ("c3", 3), ("m", 1),
    ("c3", 0), ("m", 2), ("p", 3), ("z", 1), ("p", 0), ("z", 2), ("m", 3),
    ("m", 0), ("z", 3), ("z", 0), ("g", 0), ("g", 1), ("g", 2), ("g", 3),
)


def slot_of(offset):
    return OFFSETS.index(4 if offset == -4 else offset)


def gelu_parts(preact):
    inner = tanh_scale * (preact + cubic_coeff * preact * preact * preact)
    hyper = jnp.tanh(inner)
    activated = 0.5 * preact * (1.0 + hyper)
    derivative = 0.5 * (1.0 + hyper) + 0.5 * preact * (1.0 - hyper * hyper) * tanh_scale * (
        1.0 + 3.0 * cubic_coeff * preact * preact
    )
    return (activated, derivative)


def contract(left, right, left_dim, right_dim):
    return lax.dot_general(
        left, right, (((left_dim,), (right_dim,)), ((), ())), preferred_element_type=jnp.float32
    )


def rows_of(value):
    return value.reshape((-1, value.shape[-1]))


def kernel(
    act_hbm, up_hbm, down_hbm, cot_hbm,
    out_hbm, in_grad_hbm, up_grad_hbm, down_grad_hbm,
    tok, act_t, w_up, w_down, acc0, s1, r1, acc2, s2, r2, acc3, s3, r3, acc4, s4, r4,
    hp, part, q0, ky, sy, ry, own, ds, rd, up_out, down_out, small_out,
    load_sem, store_sem, send_sem, recv_sem,
):
    bf16, f32 = jnp.bfloat16, jnp.float32
    width = tok.shape[-1]
    half = width // 2
    depth, row, z = lax.axis_index("depth"), lax.axis_index("row"), lax.axis_index("col")
    yl, k = depth // 2, depth % 2
    x, yh = row // 4, row % 4
    f1x, f2x = (x + x // 2) % 2, x // 2
    f1y, f2y = (yh + yh // 2) % 2, yh // 2
    p1x, p2x = {"row": (x + 1 - 2 * (x % 2)) * 4 + yh}, {"row": (3 - x) * 4 + yh}
    p1y, p2y = {"row": x * 4 + yh + 1 - 2 * (yh % 2)}, {"row": x * 4 + 3 - yh}
    sibling, ypartner = {"depth": yl * 2 + 1 - k}, {"depth": (1 - yl) * 2 + k}

    def along(offset):
        return {"col": (z + offset + 8) % 8}

    partners = [sibling, ypartner, p1x, p2x, p1y, p2y] + [along(o) for o in OFFSETS[1:]]

    started, kinds = [], []

    def send(kind, src, dst, device):
        n = len(started)
        if kind not in kinds:
            kinds.append(kind)
        copy = pltpu.make_async_remote_copy(
            src_ref=src, dst_ref=dst, send_sem=send_sem.at[kinds.index(kind)],
            recv_sem=recv_sem.at[n],
            device_id=device, device_id_type=pl.DeviceIdType.MESH,
        )
        copy.start()
        started.append(copy)
        return copy

    loads = [
        pltpu.make_async_copy(act_hbm, tok.at[0, 0, k, yl], load_sem.at[0]),
        pltpu.make_async_copy(cot_hbm, tok.at[1, 0, k, yl], load_sem.at[1]),
        pltpu.make_async_copy(up_hbm, w_up, load_sem.at[2]),
        pltpu.make_async_copy(down_hbm, w_down, load_sem.at[3]),
    ]
    for load in loads:
        load.start()
    barrier = pltpu.get_barrier_semaphore()
    for device in partners:
        pl.semaphore_signal(barrier, inc=1, device_id=device, device_id_type=pl.DeviceIdType.MESH)
    pl.semaphore_wait(barrier, len(partners))

    flow, across, shared = {}, {}, {}

    def block(slot, a=slice(None)):
        return tok.at[a, slot, k, yl]

    def hop(offset, way, a=slice(None)):
        target = offset - way
        flow[target] = flow.get(target, []) + [
            send("hop", block(slot_of(offset), a), block(slot_of(target), a), along(way))
        ]

    def cross(slot):
        across[slot] = send("cross", block(slot), block(slot), ypartner)

    def arrive(offset):
        for copy in flow[offset]:
            copy.wait_recv()

    def share(c):
        for slot in (2 * c, 2 * c + 1):
            across[slot].wait_recv()
        mine = tok.at[:, 2 * c : 2 * c + 2, k]
        shared[c] = send("share", mine, mine, sibling)

    wave = {}

    def flip_tokens(c):
        act_t[:, c * 8 * BLK : (c + 1) * 8 * BLK] = rows_of(tok[0, 2 * c : 2 * c + 2]).T

    def reduce1(c):
        shared[c].wait_recv()
        for a in range(2):
            i, f = 2 * c + a, (f1x, f2x)[a]
            rows = rows_of(tok[a, 2 * c : 2 * c + 2])
            value = contract(rows, w_up[...], 1, 0) if a == 0 else contract(rows, w_down[...], 1, 1)
            acc0[i] = value.reshape(acc0.shape[1:])
            s1[i] = (acc0[i, 1 - f] if a == 0 else acc0[i, :, 1 - f]).astype(bf16)
            wave[c, a] = send("s1", s1.at[i], r1.at[i], (p1x, p2x)[a])

    def reduce2(c):
        for a in range(2):
            i, f, g = 2 * c + a, (f1x, f2x)[a], (f2x, f1x)[a]
            wave[c, a].wait_recv()

            def total(n):
                kept = acc0[i, f, n] if a == 0 else acc0[i, n, f]
                return kept + r1[i, n].astype(f32)

            value = total(1 - g).astype(bf16)
            s2[i, :, 0] = value[..., :half]
            s2[i, :, 1] = value[..., half:]
            wave[c, a] = send("s2", s2.at[i], r2.at[i], (p2x, p1x)[a])
            value = total(g)
            acc2[i, :, 0] = value[..., :half]
            acc2[i, :, 1] = value[..., half:]

    def reduce3(c):
        for a in range(2):
            i, f = 2 * c + a, (f1y, f2y)[a]
            wave[c, a].wait_recv()

            def total(n):
                if a == 0:
                    return acc2[i, n] + r2[i, n].astype(f32)
                return acc2[i, :, n] + r2[i, :, n].astype(f32)

            s3[i] = total(1 - f).astype(bf16)
            wave[c, a] = send("s3", s3.at[i], r3.at[i], (p1y, p2y)[a])
            acc3[i] = total(f)

    def reduce4(c):
        for a in range(2):
            i, f = 2 * c + a, (f2y, f1y)[a]
            wave[c, a].wait_recv()
            s4[i] = acc3[i, 1 - f] + r3[i, 1 - f].astype(f32)
            wave[c, a] = send("s4", s4.at[i], r4.at[i], (p2y, p1y)[a])
            acc4[i] = acc3[i, f] + r3[i, f].astype(f32)

    def double(c, step):
        for a in range(2):
            if step > 0:
                wave[c, a].wait_recv()
            if step == 0:
                region, device = hp.at[c, a, f1x, f2x, f1y, f2y], (p2y, p1y)[a]
            elif step == 1:
                region = hp.at[c, a, f1x, f2x, f1y] if a == 0 else hp.at[c, a, f1x, f2x, :, f2y]
                device = (p1y, p2y)[a]
            elif step == 2:
                region, device = hp.at[c, a, f1x, f2x], (p2x, p1x)[a]
            else:
                region = hp.at[c, a, f1x] if a == 0 else hp.at[c, a, :, f2x]
                device = (p1x, p2x)[a]
            wave[c, a] = send(("d0", "d1", "d2", "d3")[step], region, region, device)

    def activate(c):
        wave[c, 0].wait_recv()
        wave[c, 1].wait_recv()
        activated, derivative = gelu_parts(acc4[2 * c] + r4[2 * c])
        hp[c, 0, f1x, f2x, f1y, f2y] = activated.astype(bf16)
        backed = acc4[2 * c + 1] + r4[2 * c + 1]
        hp[c, 1, f1x, f2x, f1y, f2y] = (backed * derivative).astype(bf16)
        double(c, 0)

    pair, cut, scattered = {}, {}, []

    def project(c):
        for a in range(2):
            wave[c, a].wait_recv()
            low, high = rows_of(hp[c, a, :, :, :, 0]), rows_of(hp[c, a, :, :, :, 1])
            rows = jnp.concatenate([low, high], axis=1)
            value = contract(rows, w_down[...], 1, 0) if a == 0 else contract(rows, w_up[...], 1, 1)
            part[c, a] = value.reshape(part.shape[2:])
            pair[c, a] = send("part", part.at[c, a, :, 1 - k], q0.at[c, a], sibling)

    def merge(c):
        for a in range(2):
            pair[c, a].wait_recv()
            sy[c, a] = (part[c, a, :, k, 1 - yl] + q0[c, a, :, 1 - yl]).astype(bf16)
        cut[c] = send("sy", sy.at[c], ry.at[c], ypartner)
        for a in range(2):
            ky[c, a] = part[c, a, :, k, yl] + q0[c, a, :, yl]

    def scatter(c):
        cut[c].wait_recv()
        for s in (1, 0):
            slot = 2 * c + s
            value = ky[c, :, s] + ry[c, :, s].astype(f32)
            if slot == 0:
                own[...] = value
            else:
                ds[slot] = value.astype(bf16)
                scattered.append(send("ds", ds.at[slot], rd.at[slot], along(OFFSETS[slot])))

    stores = []

    def store(src, dst):
        stores.append(pltpu.make_async_copy(src, dst, store_sem.at[len(stores)]))
        stores[-1].start()

    def up_grad(h):
        cols = slice(h * half, (h + 1) * half)
        right = rows_of(hp[:, 1, :, :, :, h])
        up_out[:, cols] = contract(act_t[...], right, 1, 0).astype(bf16)
        store(up_out.at[:, cols], up_grad_hbm.at[:, cols])

    def down_grad(h):
        rows = slice(h * half, (h + 1) * half)
        left, right = rows_of(hp[:, 0, :, :, :, h]), rows_of(tok[1])
        down_out[rows, :] = contract(left, right, 0, 0).astype(bf16)
        store(down_out.at[rows], down_grad_hbm.at[rows])

    def begin():
        loads[0].wait()
        loads[1].wait()
        hop(0, 1)
        hop(0, -1)
        cross(0)
        hop(0, 2)
        hop(0, -2)

    def pass_on(offset):
        arrive(offset)
        if offset == 4:
            arrive(-4)
        if offset in (2, -2):
            way = -offset // 2
            hop(offset, way)
            hop(offset, 2 * way, 0 if way == 1 else 1)
        cross(slot_of(offset))

    def grads(n):
        (up_grad, down_grad)[n // 2](n % 2)

    stages = {
        "y": pass_on, "s": share, "ta": flip_tokens, "r1": reduce1, "r2": reduce2, "r3": reduce3, "r4": reduce4,
        "act": activate, "c1": lambda c: double(c, 1), "c2": lambda c: double(c, 2),
        "c3": lambda c: double(c, 3), "p": project, "m": merge, "z": scatter, "g": grads,
    }
    begin()
    loads[2].wait()
    loads[3].wait()
    for stage, index in ORDER:
        stages[stage](index)
    for copy in scattered:
        copy.wait_recv()
    for a, ref in ((0, out_hbm), (1, in_grad_hbm)):
        total = own[a]
        for slot in range(1, 8):
            total = total + rd[slot, a].astype(f32)
        small_out[a] = total.astype(bf16)
        store(small_out.at[a], ref)
    sent = {
        "hop": tok.at[:, 0:7, 0, 0], "cross": tok.at[:, :, 0, 0], "share": tok.at[:, :, 0],
        "s1": s1, "s2": s2, "s3": s3, "s4": s4, "d0": hp.at[:, :, 0, 0, 0, 0],
        "d1": hp.at[:, :, 0, 0, 0], "d2": hp.at[:, :, 0, 0], "d3": hp.at[:, :, 0],
        "part": q0, "sy": sy, "ds": ds.at[1:8],
    }
    for kind, ref in sent.items():
        pltpu.make_async_copy(ref, ref, send_sem.at[kinds.index(kind)]).wait()
    for copy in stores:
        copy.wait()


KINDS, COPIES = 14, 128


def place(*refs):
    arrays, results, buffers, load_sem, store_sem = refs[:4], refs[4:8], refs[8:12], refs[12], refs[13]
    loads, stores = [], []
    for src, dst, buffer in zip(arrays, results, buffers):
        rows = src.shape[0]
        step = min(rows, 256)
        for first in range(0, rows, step):
            n, part = len(loads), pl.ds(first, step)
            loads.append(pltpu.make_async_copy(src.at[part], buffer.at[part], load_sem.at[n]))
            stores.append(pltpu.make_async_copy(buffer.at[part], dst.at[part], store_sem.at[n]))
    for load in loads:
        load.start()
    for load, store in zip(loads, stores):
        load.wait()
        store.start()
    for store in stores:
        store.wait()


def shards(activations, weight_up, weight_down, out_grad):
    width, hidden = weight_up.shape
    bf16, f32 = jnp.bfloat16, jnp.float32
    assert activations.shape[0] == BLK and width == hidden

    def vmem(lead, kind):
        return pltpu.VMEM(lead + (BLK, width), kind)

    def halves(lead, kind):
        return pltpu.VMEM(lead + (BLK, hidden // 2), kind)

    pieces = 2 * CHUNKS
    scratch = [
        vmem((2, 8, 2, 2), bf16),
        pltpu.VMEM((width, 8 * CHUNKS * BLK), bf16),
        pltpu.VMEM((width, hidden), bf16), pltpu.VMEM((width, hidden), bf16),
        vmem((pieces, 2, 2, 2), f32), vmem((pieces, 2, 2), bf16), vmem((pieces, 2, 2), bf16),
        halves((pieces, 2, 2), f32), halves((pieces, 2, 2), bf16), halves((pieces, 2, 2), bf16),
        halves((pieces, 2), f32), halves((pieces, 2), bf16), halves((pieces, 2), bf16),
        halves((pieces,), f32), halves((pieces,), f32), halves((pieces,), f32),
        halves((CHUNKS, 2, 2, 2, 2, 2), bf16),
        vmem((CHUNKS, 2, 2, 2, 2), f32), vmem((CHUNKS, 2, 2, 2), f32),
        vmem((CHUNKS, 2, 2), f32), vmem((CHUNKS, 2, 2), bf16), vmem((CHUNKS, 2, 2), bf16),
        vmem((2,), f32), vmem((8, 2), bf16), vmem((8, 2), bf16),
        pltpu.VMEM((width, hidden), bf16), pltpu.VMEM((width, hidden), bf16), vmem((2,), bf16),
        pltpu.SemaphoreType.DMA((4,)), pltpu.SemaphoreType.DMA((6,)),
        pltpu.SemaphoreType.DMA((KINDS,)), pltpu.SemaphoreType.DMA((COPIES,)),
    ]
    small = jax.ShapeDtypeStruct(activations.shape, bf16)
    large = jax.ShapeDtypeStruct(weight_up.shape, bf16)
    results = pl.pallas_call(
        kernel,
        out_shape=(small, small, large, large),
        in_specs=[pl.BlockSpec(memory_space=pltpu.HBM)] * 4,
        out_specs=[pl.BlockSpec(memory_space=pltpu.HBM)] * 4,
        scratch_shapes=scratch,
        compiler_params=pltpu.CompilerParams(
            collective_id=0, has_side_effects=True, vmem_limit_bytes=VMEM_MIB * 1024 * 1024
        ),
        cost_estimate=pl.CostEstimate(
            flops=12 * 512 * width * hidden, bytes_accessed=8 * width * hidden, transcendentals=0
        ),
        name="layer",
    )(activations, weight_up, weight_down, out_grad)
    out, in_grad, up_grad, down_grad = results
    up_grad, down_grad, out, in_grad = pl.pallas_call(
        place,
        out_shape=(large, large, small, small),
        in_specs=[pl.BlockSpec(memory_space=pltpu.HBM)] * 4,
        out_specs=[pl.BlockSpec(memory_space=pltpu.HBM)] * 4,
        scratch_shapes=[pltpu.VMEM(result.shape, bf16) for result in (large, large, small, small)]
        + [pltpu.SemaphoreType.DMA((8,)), pltpu.SemaphoreType.DMA((8,))],
        compiler_params=pltpu.CompilerParams(vmem_limit_bytes=VMEM_MIB * 1024 * 1024),
        name="place",
    )(up_grad, down_grad, out, in_grad)
    return out, in_grad, up_grad, down_grad


VMEM_MIB = 60


def solution(mesh):
    placed = (
        P(("depth", "col"), "row"),
        P("row", ("depth", "col")),
        P(("depth", "col"), "row"),
        P(("depth", "col"), "row"),
    )
    return jax.shard_map(
        shards,
        mesh=mesh,
        in_specs=placed,
        out_specs=(
            P(("depth", "col"), "row"),
            P(("depth", "col"), "row"),
            P("row", ("depth", "col")),
            P(("depth", "col"), "row"),
        ),
        check_vma=False,
    )
```
